32 devices in a mesh: seq: 8 (over z, y), head: 4 (over x, core).
Axes of the slice: x: 2, y: 2, z: 4, core: 2. Of those that a mesh axis runs over, the one named last changes fastest.
Arguments:
- node_features: bfloat16 [12288, 512], P('seq'), may hold values from -136 to 136
- gain: float32 [512], replicated, may hold values from 0.5 to 1.5
- w_qkv: bfloat16 [3, 512, 512], P(None, None, 'head'), may hold values from -3.1 to 3.1
- d_out: bfloat16 [12288, 512], P('seq'), may hold values from -6 to 6
- pattern: int32 [96, 3], replicated, may hold values from 0 to 95, as said below
- counts: int32 [96], P('seq'), may hold values from 1 to 3
Outputs:
- layer_output: bfloat16 [12288, 512], P('seq', 'head')
- grad_input: bfloat16 [12288, 512], P('seq', 'head')
- grad_weights: float32 [3, 512, 512], P(None, 'seq', 'head')
The draws below stay inside these ranges and needn't reach their ends.
Inputs may be any that keep to these rules, and one draw needn't show every extreme that they name: `pattern`: block id p lives on index p // 12 of seq. Among the 36 entries of the query blocks of one index of seq (live or not), at most 6 name blocks living on any one index of seq, and on every index some index is named exactly 6 times.
All inputs are finite; a program needn't handle non-finite values.
Results may differ from the reference program's by a relative error of at most 0.012.
The reference program's roundings to bfloat16 on the way count: a program that leaves them out, or rounds other values in their place, can miss the bound.
Values may be sent and summed in bfloat16 or wider, within the bound.
A program may use at most 128 MiB of HBM per device.

```python
import math
import jax
import jax.numpy as jnp
from jax import lax

D = 512
HEADS = 8
HEAD_DIM = 64
BLOCK = 128
EXPD = 3
BLK_DEV = 12
NBLOCKS = 96
NODES = 12288
CAP = 6
N_SEQ = 8


def spread_scale(key, shape, lower, upper):
    return jnp.exp(jax.random.uniform(key, shape, jnp.float32, math.log(lower), math.log(upper)))


def draw_node_features(key, part):
    pieces = jax.random.split(key, 3)
    base = jnp.clip(jax.random.normal(pieces[0], (NODES, D), jnp.float32), -4.0, 4.0)
    row_scale = spread_scale(pieces[1], (NODES, 1), 0.5, 5.0)
    col_scale = spread_scale(pieces[2], (1, D), 0.5, 5.0)
    return (base * row_scale * col_scale).astype(jnp.bfloat16)


def draw_w_qkv(key, part):
    member = jnp.arange(3)[:, None, None]
    normal = jnp.clip(jax.random.normal(key, (3, D, D), jnp.float32), -4.0, 4.0) / math.sqrt(D)
    return jnp.where(member < 2, 1.5 * normal, normal).astype(jnp.bfloat16)


def one_device(sub):
    pieces = jax.random.split(sub, 4)
    forced = jax.random.randint(pieces[0], (), 0, N_SEQ)
    others = (jnp.arange((N_SEQ - 1) * CAP) // CAP + forced + 1) % N_SEQ
    chosen = jax.random.permutation(pieces[1], others)[:BLK_DEV * EXPD - CAP]
    owners = jnp.concatenate([jnp.zeros((CAP,), jnp.int32) + forced, chosen.astype(jnp.int32)])
    owners = jax.random.permutation(pieces[2], owners)
    in_owner = jax.random.randint(pieces[3], (BLK_DEV * EXPD,), 0, BLK_DEV)
    return owners * BLK_DEV + in_owner


def draw_pattern(key, part):
    return jax.vmap(one_device)(jax.random.split(key, N_SEQ)).reshape(NBLOCKS, EXPD).astype(jnp.int32)


def set_ends(drawn, stream_key, smallest, largest):
    shape = drawn.shape
    spot = [jax.random.randint(jax.random.fold_in(stream_key, axis), (), 0, shape[axis]) for axis in range(len(shape))]
    drawn = drawn.at[tuple(spot)].set(smallest)
    longest = shape.index(max(shape))
    spot[longest] = (spot[longest] + 1) % shape[longest]
    return drawn.at[tuple(spot)].set(largest)


def block_levels(key, dims, cuts, low, largest):
    def one(dim, blocks):
        draws = jax.random.uniform(jax.random.fold_in(jax.random.fold_in(key, 6), dim), (blocks,), jnp.float32, low / len(cuts), largest / len(cuts))
        return jnp.repeat(jnp.exp(draws), dims[dim] // blocks).reshape((-1,) + (1,) * (len(dims) - dim - 1))

    level = one(*cuts[0])
    for cut in cuts[1:]:
        level = level * one(*cut)
    return level


def centred(stream_key, dims, scale, most, cuts=(), held_as=jnp.bfloat16):
    entries = scale * jax.random.normal(stream_key, dims, jnp.float32)
    if cuts:
        entries = entries * block_levels(stream_key, dims, cuts, -0.22, 0.18)
    return jnp.clip(entries, -most, most).astype(held_as)


def setup_inputs(seed: int = 0) -> dict:
    keys = jax.random.split(jax.random.key(seed), 7)
    node_features = draw_node_features(jax.random.fold_in(keys[6], 71), 0)
    gain = jnp.clip(1.0 + 0.1 * jax.random.normal(keys[1], (D,), jnp.float32), 0.5, 1.5)
    w_qkv = draw_w_qkv(jax.random.fold_in(keys[6], 71), 0)
    d_out = centred(keys[3], (NODES, D), 1.0, 6.0, ((0, 8),))
    pattern = draw_pattern(jax.random.fold_in(keys[6], 71), 0)
    counts = set_ends(jax.random.randint(keys[5], (NBLOCKS,), 1, EXPD + 1), jax.random.fold_in(keys[5], 1), 1, EXPD).astype(jnp.int32)
    return {"node_features": node_features, "gain": gain, "w_qkv": w_qkv, "d_out": d_out, "pattern": pattern, "counts": counts}


EPS = 1e-06

def reference(node_features, gain, w_qkv, d_out, pattern, counts):
    node_count = node_features.shape[0]
    block_total = node_count // BLOCK
    x_float = node_features.astype(jnp.float32)
    gain_float = gain.astype(jnp.float32)
    inv_rms = lax.rsqrt(lax.optimization_barrier(jnp.mean(x_float * x_float, axis=1, keepdims=True)) + EPS)
    normed = (x_float * inv_rms * gain_float).astype(jnp.bfloat16)
    projected = [jnp.dot(normed, w_qkv[member], preferred_element_type=jnp.float32).astype(jnp.bfloat16) for member in range(3)]
    shape_heads = (block_total, BLOCK, HEADS, HEAD_DIM)
    queries = projected[0].reshape(shape_heads)
    keys_all = projected[1].reshape(shape_heads)
    values_all = projected[2].reshape(shape_heads)
    score_scale = 1.0 / math.sqrt(HEAD_DIM)
    listed = jnp.concatenate([jnp.arange(block_total, dtype=jnp.int32)[:, None], pattern.astype(jnp.int32)], axis=1)
    live = jnp.concatenate([jnp.ones((block_total, 1), bool), jnp.arange(EXPD)[None, :] < counts[:, None]], axis=1)
    grad_out = d_out.reshape(shape_heads)
    x_heads = x_float.reshape(shape_heads)

    def block_step(carried, index):
        grad_keys, grad_values = carried
        listed_ids = listed[index]
        key_block = keys_all[listed_ids].astype(jnp.float32)
        value_block = values_all[listed_ids].astype(jnp.float32)
        query_block = queries[index].astype(jnp.float32)
        scores = jnp.einsum('qhe,tkhe->hqtk', query_block, key_block) * score_scale
        scores = jnp.where(live[index][None, None, :, None], scores, -jnp.inf)
        row_peak = lax.optimization_barrier(jnp.max(scores, axis=(2, 3), keepdims=True))
        powers = jnp.exp(scores - row_peak)
        attention = powers / lax.optimization_barrier(jnp.sum(powers, axis=(2, 3), keepdims=True))
        attention_low = lax.optimization_barrier(attention.astype(jnp.bfloat16)).astype(jnp.float32)
        attended = jnp.einsum('hqtk,tkhe->qhe', attention_low, value_block)
        out_block = (x_heads[index] + attended).astype(jnp.bfloat16)
        grad_block = grad_out[index].astype(jnp.float32)
        grad_attention = jnp.einsum('qhe,tkhe->hqtk', grad_block, value_block)
        row_dot = jnp.transpose(lax.optimization_barrier(jnp.sum(grad_block * attended, axis=2)), (1, 0))
        grad_scores = attention * (grad_attention - row_dot[:, :, None, None]) * score_scale
        grad_scores = lax.optimization_barrier(grad_scores.astype(jnp.bfloat16)).astype(jnp.float32)
        grad_query = jnp.einsum('hqtk,tkhe->qhe', grad_scores, key_block).astype(jnp.bfloat16)
        grad_keys = grad_keys.at[listed_ids].add(jnp.einsum('hqtk,qhe->tkhe', grad_scores, query_block))
        grad_values = grad_values.at[listed_ids].add(jnp.einsum('hqtk,qhe->tkhe', attention_low, grad_block))
        return ((grad_keys, grad_values), (out_block, grad_query))
    zero_grads = jnp.zeros(shape_heads, jnp.float32)
    (grad_keys, grad_values), (out_blocks, grad_queries) = lax.scan(block_step, (zero_grads, zero_grads), jnp.arange(block_total, dtype=jnp.int32))
    layer_output = out_blocks.reshape(node_count, D)
    grads = (grad_queries.reshape(node_count, D), grad_keys.reshape(node_count, D).astype(jnp.bfloat16), grad_values.reshape(node_count, D).astype(jnp.bfloat16))
    grad_normed = jnp.dot(grads[0], w_qkv[0].T, preferred_element_type=jnp.float32)
    grad_normed = grad_normed + jnp.dot(grads[1], w_qkv[1].T, preferred_element_type=jnp.float32)
    grad_normed = grad_normed + jnp.dot(grads[2], w_qkv[2].T, preferred_element_type=jnp.float32)
    row_term = lax.optimization_barrier(jnp.mean(x_float * gain_float * grad_normed, axis=1, keepdims=True))
    cubed = inv_rms * inv_rms * inv_rms
    grad_input = (d_out.astype(jnp.float32) + inv_rms * gain_float * grad_normed - x_float * cubed * row_term).astype(jnp.bfloat16)
    grad_weights = jnp.stack([jnp.dot(normed.T, member, preferred_element_type=jnp.float32) for member in grads]) / math.sqrt(node_count)
    return (layer_output, grad_input, grad_weights)
```

```python
import functools
import math

import jax
import jax.numpy as jnp
from jax import lax
from jax.experimental import pallas as pl
from jax.experimental.pallas import tpu as pltpu
from jax.sharding import PartitionSpec as P

HEAD_DIM = 64
BLOCK = 128
EXPD = 3
CHUNK = 256


EPS = 1e-06
F32 = jnp.float32
BF16 = jnp.bfloat16
VMEM_LIMIT = 50 * 1024 * 1024

CONTRACT_COLS = (((1,), (1,)), ((), ()))
CONTRACT_ROWS = (((0,), (0,)), ((), ()))


def rows_of(index, size):
    return pl.ds(pl.multiple_of(index * size, size), size)


def join_weights(w_ref, joined, cols):
    for member in range(3):
        joined[:, member * cols : (member + 1) * cols] = w_ref[member]


def project_kernel(sent_from, x_ref, gain_ref, w_ref, normed_ref, q_ref, kv_ref, out_ref, joined):
    cols = w_ref.shape[2]
    per_chunk = CHUNK // BLOCK
    join_weights(w_ref, joined, cols)

    def project(step, carry):
        rows = rows_of(step, CHUNK)
        x = x_ref[rows, :].astype(F32)
        inv_rms = lax.rsqrt(jnp.mean(x * x, axis=1, keepdims=True) + EPS)
        normed = (x * inv_rms * gain_ref[...]).astype(BF16)
        normed_ref[rows, :] = normed
        made = jnp.dot(normed, joined[...], preferred_element_type=F32).astype(BF16)
        q_ref[rows, :] = made[:, :cols]
        kv_ref[pl.ds(step * per_chunk, per_chunk)] = made[:, cols:].reshape(
            per_chunk, BLOCK, 2 * cols
        )
        return carry

    lax.fori_loop(0, x_ref.shape[0] // CHUNK, project, 0)

    def pack(slot, carry):
        out_ref[slot] = kv_ref[sent_from[slot]]
        return carry

    lax.fori_loop(0, out_ref.shape[0], pack, 0)


def attend_kernel(
    head, slots, counts, q_ref, kv_ref, slot_ref, x_ref, d_ref, layer_ref, gq_ref, own_ref, back_ref
):
    cols = q_ref.shape[1]
    heads_here = cols // HEAD_DIM
    scale = 1.0 / math.sqrt(HEAD_DIM)
    keys_all = (1 + EXPD) * BLOCK
    lane_head = lax.broadcasted_iota(jnp.int32, (BLOCK, cols), 1) // HEAD_DIM
    key_place = lax.broadcasted_iota(jnp.int32, (1, keys_all), 1)

    def spread(value):
        return jnp.concatenate(
            [jnp.where(lane_head == h, value, jnp.zeros_like(value)) for h in range(heads_here)],
            axis=0,
        )

    def merge(value):
        made = value[:BLOCK]
        for h in range(1, heads_here):
            made = jnp.where(lane_head == h, value[h * BLOCK : (h + 1) * BLOCK], made)
        return made

    def block_step(block, carry):
        rows = rows_of(block, BLOCK)
        places = [slots[block * EXPD + j] for j in range(EXPD)]
        own = kv_ref[block]
        listed = jnp.concatenate([own] + [slot_ref[place] for place in places], axis=0)
        keys = listed[:, :cols]
        values = listed[:, cols:]
        queries = spread(q_ref[rows, :])
        grads = spread(d_ref[rows, :])
        scores = lax.dot_general(queries, keys, CONTRACT_COLS, preferred_element_type=F32) * scale
        scores = jnp.where(key_place < (counts[block] + 1) * BLOCK, scores, -jnp.inf)
        powers = jnp.exp(scores - jnp.max(scores, axis=1, keepdims=True))
        attention = powers * (1.0 / jnp.sum(powers, axis=1, keepdims=True))
        low = attention.astype(BF16)
        attended = jnp.dot(low, values, preferred_element_type=F32)
        layer_ref[rows, :] = (x_ref[rows, :].astype(F32) + merge(attended)).astype(BF16)
        grad_attention = lax.dot_general(grads, values, CONTRACT_COLS, preferred_element_type=F32)
        row_dot = jnp.sum(grads.astype(F32) * attended, axis=1, keepdims=True)
        grad_scores = (attention * (grad_attention - row_dot) * scale).astype(BF16)
        gq_ref[rows, :] = merge(jnp.dot(grad_scores, keys, preferred_element_type=F32)).astype(BF16)
        grad_keys = lax.dot_general(grad_scores, queries, CONTRACT_ROWS, preferred_element_type=F32)
        grad_values = lax.dot_general(low, grads, CONTRACT_ROWS, preferred_element_type=F32)
        own_ref[block] = jnp.concatenate([grad_keys[:BLOCK], grad_values[:BLOCK]], axis=1)
        for j, place in enumerate(places):
            part = slice((j + 1) * BLOCK, (j + 2) * BLOCK)
            back_ref[place] = jnp.concatenate([grad_keys[part], grad_values[part]], axis=1).astype(
                BF16
            )
        return carry

    lax.fori_loop(0, kv_ref.shape[0], block_step, 0)


def weight_kernel(
    sent_from,
    filled,
    own_ref,
    back_ref,
    gq_ref,
    normed_ref,
    x_ref,
    gain_ref,
    w_ref,
    gn_ref,
    term_ref,
    gw_ref,
    joined,
    total,
    sums,
    *,
    node_count,
):
    cols = w_ref.shape[2]
    width = w_ref.shape[1]
    row_count = x_ref.shape[0]
    per_chunk = CHUNK // BLOCK
    join_weights(w_ref, joined, cols)
    total[...] = own_ref[...]
    sums[...] = jnp.zeros_like(sums)

    def gather(slot, carry):
        @pl.when(filled[slot] > 0)
        def _():
            place = sent_from[slot]
            total[place] = total[place] + back_ref[slot].astype(F32)

        return carry

    lax.fori_loop(0, back_ref.shape[0], gather, 0)

    def chunk_step(step, carry):
        rows = rows_of(step, CHUNK)
        grad_kv = total[pl.ds(step * per_chunk, per_chunk)].reshape(CHUNK, 2 * cols).astype(BF16)
        grads = jnp.concatenate([gq_ref[rows, :], grad_kv], axis=1)
        grad_normed = lax.dot_general(grads, joined[...], CONTRACT_COLS, preferred_element_type=F32)
        for part in range(width // cols):
            gn_ref[part, rows, :] = grad_normed[:, part * cols : (part + 1) * cols].astype(BF16)
        term = jnp.sum(
            x_ref[rows, :].astype(F32) * gain_ref[...] * grad_normed, axis=1, keepdims=True
        )
        for inner in range(per_chunk):
            piece = jnp.broadcast_to(term[inner * BLOCK : (inner + 1) * BLOCK], (BLOCK, BLOCK))
            term_ref[step * per_chunk + inner] = piece.T[:8]
        sums[...] += lax.dot_general(
            normed_ref[rows, :], grads, CONTRACT_ROWS, preferred_element_type=F32
        )
        return carry

    lax.fori_loop(0, row_count // CHUNK, chunk_step, 0)
    seq_count = gw_ref.shape[0]
    share = width // seq_count
    factor = 1.0 / math.sqrt(node_count)
    for peer in range(seq_count):
        for member in range(3):
            gw_ref[peer, member] = (
                sums[peer * share : (peer + 1) * share, member * cols : (member + 1) * cols]
                * factor
            ).astype(BF16)


def input_kernel(head, gn_ref, term_ref, x_ref, mine_ref, d_ref, gain_ref, out_ref):
    width = x_ref.shape[1]

    def block_step(block, carry):
        rows = rows_of(block, BLOCK)
        x = x_ref[rows, :].astype(F32)
        inv_rms = lax.rsqrt(jnp.mean(x * x, axis=1, keepdims=True) + EPS)
        grad = gn_ref[0, rows, :].astype(F32)
        for part in range(1, gn_ref.shape[0]):
            grad = grad + gn_ref[part, rows, :].astype(F32)
        row = term_ref[pl.ds(block, 1), :]
        term = jnp.broadcast_to(row, (BLOCK, BLOCK)).T[:, :1] * (1.0 / width)
        cubed = inv_rms * inv_rms * inv_rms
        out_ref[rows, :] = (
            d_ref[rows, :].astype(F32)
            + inv_rms * gain_ref[...] * grad
            - mine_ref[rows, :].astype(F32) * (cubed * term)
        ).astype(BF16)
        return carry

    lax.fori_loop(0, x_ref.shape[0] // BLOCK, block_step, 0)


def whole(shape):
    return pl.BlockSpec(shape, lambda i, *refs: (0,) * len(shape))


def run(kernel, scalars, args, outs, scratch=(), columns=(), col_count=128):
    if columns and col_count % 128:
        args = [
            lax.dynamic_slice_in_dim(value, scalars[0][0] * col_count, col_count, 1)
            if place in columns
            else value
            for place, value in enumerate(args)
        ]
        columns = ()

    def spec(place, value):
        if place in columns:
            return pl.BlockSpec(
                (value.shape[0], col_count), lambda i, head, *refs: (0, head[0])
            )
        return whole(value.shape)

    return pl.pallas_call(
        kernel,
        out_shape=outs,
        grid_spec=pltpu.PrefetchScalarGridSpec(
            num_scalar_prefetch=len(scalars),
            grid=(1,),
            in_specs=[spec(place, value) for place, value in enumerate(args)],
            out_specs=jax.tree.map(lambda out: whole(out.shape), outs),
            scratch_shapes=list(scratch),
        ),
        compiler_params=pltpu.CompilerParams(vmem_limit_bytes=VMEM_LIMIT),
    )(*scalars, *args)


def shards(node_features, gain, w_qkv, d_out, pattern, counts):
    seq_count = lax.axis_size("seq")
    my_index = lax.axis_index("seq")
    row_count, width = node_features.shape
    block_count = row_count // BLOCK
    col_count = w_qkv.shape[2]
    head_count = width // col_count
    slot_count = block_count * EXPD
    capacity = max(2, 3 * slot_count // (2 * seq_count))
    slots_all = seq_count * capacity
    kv_width = 2 * col_count
    head = lax.axis_index("head").astype(jnp.int32).reshape(1)
    gain_row = gain.reshape(1, width)
    shape = jax.ShapeDtypeStruct

    owners = (pattern // block_count).reshape(seq_count, slot_count)
    in_owner = (pattern % block_count).reshape(seq_count, slot_count)
    before = jnp.arange(slot_count)[:, None] > jnp.arange(slot_count)[None, :]
    same = owners[:, :, None] == owners[:, None, :]
    ranks = jnp.sum((same & before[None]).astype(jnp.int32), axis=2)
    places = jnp.arange(capacity, dtype=jnp.int32)
    picked = (owners[:, None, :] == my_index) & (ranks[:, None, :] == places[None, :, None])
    sent_from = jnp.sum(jnp.where(picked, in_owner[:, None, :], 0), axis=2).reshape(-1)
    filled = jnp.any(picked, axis=2).astype(jnp.int32).reshape(-1)
    my_slots = lax.dynamic_index_in_dim(owners * capacity + ranks, my_index, 0, keepdims=False)

    normed, queries, kv_local, outgoing = run(
        project_kernel,
        (sent_from,),
        (node_features, gain_row, w_qkv),
        (
            shape((row_count, width), BF16),
            shape((row_count, col_count), BF16),
            shape((block_count, BLOCK, kv_width), BF16),
            shape((slots_all, BLOCK, kv_width), BF16),
        ),
        scratch=(pltpu.VMEM((width, 3 * col_count), BF16),),
    )
    incoming = lax.all_to_all(outgoing, "seq", split_axis=0, concat_axis=0, tiled=True)
    layer_output, grad_queries, own, returning = run(
        attend_kernel,
        (head, my_slots, counts),
        (queries, kv_local, incoming, node_features, d_out),
        (
            shape((row_count, col_count), BF16),
            shape((row_count, col_count), BF16),
            shape((block_count, BLOCK, kv_width), F32),
            shape((slots_all, BLOCK, kv_width), BF16),
        ),
        columns=(3, 4),
        col_count=col_count,
    )
    returned = lax.all_to_all(returning, "seq", split_axis=0, concat_axis=0, tiled=True)
    share = width // seq_count
    grad_parts, terms, weight_parts = run(
        functools.partial(weight_kernel, node_count=row_count * seq_count),
        (sent_from, filled),
        (own, returned, grad_queries, normed, node_features, gain_row, w_qkv),
        (
            shape((head_count, row_count, col_count), BF16),
            shape((block_count, 8, BLOCK), F32),
            shape((seq_count, 3, share, col_count), BF16),
        ),
        scratch=(
            pltpu.VMEM((width, 3 * col_count), BF16),
            pltpu.VMEM((block_count, BLOCK, kv_width), F32),
            pltpu.VMEM((width, 3 * col_count), F32),
        ),
    )
    row_terms = lax.psum(terms[:, 0, :], "head")
    grad_parts = lax.all_to_all(grad_parts, "head", split_axis=0, concat_axis=0, tiled=True)
    weight_parts = lax.all_to_all(weight_parts, "seq", split_axis=0, concat_axis=0, tiled=True)
    gain_mine = lax.dynamic_slice_in_dim(gain_row, head[0] * col_count, col_count, 1)
    grad_input = run(
        input_kernel,
        (head,),
        (grad_parts, row_terms, node_features, node_features, d_out, gain_mine),
        shape((row_count, col_count), BF16),
        columns=(3, 4),
        col_count=col_count,
    )
    grad_weights = jnp.sum(weight_parts.astype(F32), axis=0)
    return (layer_output, grad_input, grad_weights)


def solution(mesh):
    in_specs = (P("seq", None), P(), P(None, None, "head"), P("seq", None), P(), P("seq"))
    out_specs = (P("seq", "head"), P("seq", "head"), P(None, "seq", "head"))
    return jax.shard_map(shards, mesh=mesh, in_specs=in_specs, out_specs=out_specs, check_vma=False)
```

```python
import functools
import math

import jax
import jax.numpy as jnp
from jax import lax
from jax.experimental import pallas as pl
from jax.experimental.pallas import tpu as pltpu
from jax.sharding import PartitionSpec as P

HEAD_DIM = 64
BLOCK = 128
EXPD = 3
CHUNK = 256


EPS = 1e-06
F32 = jnp.float32
BF16 = jnp.bfloat16
VMEM_LIMIT = 50 * 1024 * 1024

CONTRACT_COLS = (((1,), (1,)), ((), ()))
CONTRACT_ROWS = (((0,), (0,)), ((), ()))


def rows_of(index, size):
    return pl.ds(pl.multiple_of(index * size, size), size)


def join_weights(w_ref, joined, cols):
    for member in range(3):
        joined[:, member * cols : (member + 1) * cols] = w_ref[member]


def project_kernel(sent_from, x_ref, gain_ref, w_ref, normed_ref, q_ref, kv_ref, out_ref, joined):
    cols = w_ref.shape[2]
    per_chunk = CHUNK // BLOCK
    join_weights(w_ref, joined, cols)

    def project(step, carry):
        rows = rows_of(step, CHUNK)
        x = x_ref[rows, :].astype(F32)
        inv_rms = lax.rsqrt(jnp.mean(x * x, axis=1, keepdims=True) + EPS)
        normed = (x * inv_rms * gain_ref[...]).astype(BF16)
        normed_ref[rows, :] = normed
        made = jnp.dot(normed, joined[...], preferred_element_type=F32).astype(BF16)
        q_ref[rows, :] = made[:, :cols]
        kv_ref[pl.ds(step * per_chunk, per_chunk)] = made[:, cols:].reshape(
            per_chunk, BLOCK, 2 * cols
        )
        return carry

    lax.fori_loop(0, x_ref.shape[0] // CHUNK, project, 0)

    def pack(slot, carry):
        out_ref[slot] = kv_ref[sent_from[slot]]
        return carry

    lax.fori_loop(0, out_ref.shape[0], pack, 0)


def attend_kernel(
    slots, counts, q_ref, kv_ref, slot_ref, x_ref, d_ref, layer_ref, gq_ref, own_ref, back_ref
):
    cols = q_ref.shape[1]
    heads_here = cols // HEAD_DIM
    scale = 1.0 / math.sqrt(HEAD_DIM)
    keys_all = (1 + EXPD) * BLOCK
    lane_head = lax.broadcasted_iota(jnp.int32, (BLOCK, cols), 1) // HEAD_DIM
    key_place = lax.broadcasted_iota(jnp.int32, (1, keys_all), 1)

    def spread(value):
        return jnp.concatenate(
            [jnp.where(lane_head == h, value, jnp.zeros_like(value)) for h in range(heads_here)],
            axis=0,
        )

    def merge(value):
        made = value[:BLOCK]
        for h in range(1, heads_here):
            made = jnp.where(lane_head == h, value[h * BLOCK : (h + 1) * BLOCK], made)
        return made

    def block_step(block, carry):
        rows = rows_of(block, BLOCK)
        places = [slots[block * EXPD + j] for j in range(EXPD)]
        own = kv_ref[block]
        listed = jnp.concatenate([own] + [slot_ref[place] for place in places], axis=0)
        keys = listed[:, :cols]
        values = listed[:, cols:]
        queries = spread(q_ref[rows, :])
        grads = spread(d_ref[rows, :])
        scores = lax.dot_general(queries, keys, CONTRACT_COLS, preferred_element_type=F32) * scale
        scores = jnp.where(key_place < (counts[block] + 1) * BLOCK, scores, -jnp.inf)
        powers = jnp.exp(scores - jnp.max(scores, axis=1, keepdims=True))
        attention = powers * (1.0 / jnp.sum(powers, axis=1, keepdims=True))
        low = attention.astype(BF16)
        attended = jnp.dot(low, values, preferred_element_type=F32)
        layer_ref[rows, :] = (x_ref[rows, :].astype(F32) + merge(attended)).astype(BF16)
        grad_attention = lax.dot_general(grads, values, CONTRACT_COLS, preferred_element_type=F32)
        row_dot = jnp.sum(grads.astype(F32) * attended, axis=1, keepdims=True)
        grad_scores = (attention * (grad_attention - row_dot) * scale).astype(BF16)
        gq_ref[rows, :] = merge(jnp.dot(grad_scores, keys, preferred_element_type=F32)).astype(BF16)
        grad_keys = lax.dot_general(grad_scores, queries, CONTRACT_ROWS, preferred_element_type=F32)
        grad_values = lax.dot_general(low, grads, CONTRACT_ROWS, preferred_element_type=F32)
        own_ref[block] = jnp.concatenate([grad_keys[:BLOCK], grad_values[:BLOCK]], axis=1)
        for j, place in enumerate(places):
            part = slice((j + 1) * BLOCK, (j + 2) * BLOCK)
            back_ref[place] = jnp.concatenate([grad_keys[part], grad_values[part]], axis=1).astype(
                BF16
            )
        return carry

    lax.fori_loop(0, kv_ref.shape[0], block_step, 0)


def gather_kernel(
    sent_from, filled, own_ref, back_ref, gq_ref, normed_ref, grads_ref, gw_ref, total, sums, *, node_count
):
    cols = gq_ref.shape[1]
    width = normed_ref.shape[1]
    per_chunk = CHUNK // BLOCK
    sums[...] = jnp.zeros_like(sums)
    total[...] = own_ref[...]

    def gather(slot, carry):
        @pl.when(filled[slot] > 0)
        def _():
            place = sent_from[slot]
            total[place] = total[place] + back_ref[slot].astype(F32)

        return carry

    lax.fori_loop(0, back_ref.shape[0], gather, 0)

    def chunk_step(step, carry):
        rows = rows_of(step, CHUNK)
        grad_kv = total[pl.ds(step * per_chunk, per_chunk)].reshape(CHUNK, 2 * cols).astype(BF16)
        grads = jnp.concatenate([gq_ref[rows, :], grad_kv], axis=1)
        grads_ref[rows, :] = grads
        sums[...] += lax.dot_general(
            normed_ref[rows, :], grads, CONTRACT_ROWS, preferred_element_type=F32
        )
        return carry

    lax.fori_loop(0, gq_ref.shape[0] // CHUNK, chunk_step, 0)
    seq_count = gw_ref.shape[0]
    share = width // seq_count
    factor = 1.0 / math.sqrt(node_count)
    for peer in range(seq_count):
        for member in range(3):
            gw_ref[peer, member] = (
                sums[peer * share : (peer + 1) * share, member * cols : (member + 1) * cols]
                * factor
            ).astype(BF16)


def exchange_kernel(
    grads_ref,
    gw_ref,
    x_ref,
    mine_ref,
    d_ref,
    gain_ref,
    gain_mine_ref,
    w_ref,
    out_ref,
    weights_ref,
    joined,
    parts,
    arrived,
    terms,
    terms_in,
    gw_in,
    part_send,
    part_recv,
    term_send,
    term_recv,
    gw_send,
    gw_recv,
):
    cols = w_ref.shape[2]
    row_count, width = x_ref.shape
    head_count = parts.shape[0]
    seq_count = gw_ref.shape[0]
    per_chunk = CHUNK // BLOCK
    chunks = row_count // CHUNK
    head = lax.axis_index("head")
    seq = lax.axis_index("seq")
    mesh_type = pl.DeviceIdType.MESH

    def head_peer(k):
        return lax.rem(head + k, head_count)

    def seq_peer(k):
        return lax.rem(seq + k, seq_count)

    barrier = pltpu.get_barrier_semaphore()
    for k in range(1, head_count):
        pl.semaphore_signal(
            barrier, inc=1, device_id={"head": head_peer(k)}, device_id_type=mesh_type
        )
    for k in range(1, seq_count):
        pl.semaphore_signal(
            barrier, inc=1, device_id={"seq": seq_peer(k)}, device_id_type=mesh_type
        )
    pl.semaphore_wait(barrier, head_count + seq_count - 2)

    def weight_copy(k):
        return pltpu.make_async_remote_copy(
            src_ref=gw_ref.at[seq_peer(k)],
            dst_ref=gw_in.at[k - 1],
            send_sem=gw_send.at[k - 1],
            recv_sem=gw_recv.at[k - 1],
            device_id={"seq": seq_peer(k)},
            device_id_type=mesh_type,
        )

    def part_copy(k, step):
        rows = rows_of(step, CHUNK)
        return pltpu.make_async_remote_copy(
            src_ref=parts.at[head_peer(k), rows],
            dst_ref=arrived.at[k - 1, rows],
            send_sem=part_send.at[k - 1, step],
            recv_sem=part_recv.at[k - 1, step],
            device_id={"head": head_peer(k)},
            device_id_type=mesh_type,
        )

    def term_copy(k):
        return pltpu.make_async_remote_copy(
            src_ref=terms,
            dst_ref=terms_in.at[k - 1],
            send_sem=term_send.at[k - 1],
            recv_sem=term_recv.at[k - 1],
            device_id={"head": head_peer(k)},
            device_id_type=mesh_type,
        )

    for k in range(1, seq_count):
        weight_copy(k).start()
    join_weights(w_ref, joined, cols)

    def chunk_step(step, carry):
        rows = rows_of(step, CHUNK)
        grad_normed = lax.dot_general(
            grads_ref[rows, :], joined[...], CONTRACT_COLS, preferred_element_type=F32
        )
        for part in range(head_count):
            parts[part, rows, :] = grad_normed[:, part * cols : (part + 1) * cols].astype(BF16)
        for k in range(1, head_count):
            part_copy(k, step).start()
        term = jnp.sum(
            x_ref[rows, :].astype(F32) * gain_ref[...] * grad_normed, axis=1, keepdims=True
        )
        for inner in range(per_chunk):
            piece = jnp.broadcast_to(term[inner * BLOCK : (inner + 1) * BLOCK], (BLOCK, BLOCK))
            terms[step * per_chunk + inner] = piece.T[:8]
        return carry

    lax.fori_loop(0, chunks, chunk_step, 0)
    for k in range(1, head_count):
        term_copy(k).start()
    for k in range(1, seq_count):
        weight_copy(k).wait()
    total = gw_ref[seq].astype(F32)
    for k in range(1, seq_count):
        total = total + gw_in[k - 1].astype(F32)
    weights_ref[...] = total
    for k in range(1, head_count):
        term_copy(k).wait()

    def final_step(step, carry):
        rows = rows_of(step, CHUNK)
        x = x_ref[rows, :].astype(F32)
        inv_rms = lax.rsqrt(jnp.mean(x * x, axis=1, keepdims=True) + EPS)
        columns = []
        for inner in range(per_chunk):
            row = terms[step * per_chunk + inner]
            for k in range(1, head_count):
                row = row + terms_in[k - 1, step * per_chunk + inner]
            columns.append(jnp.broadcast_to(row[:1], (BLOCK, BLOCK)).T[:, :1])
        term = jnp.concatenate(columns, axis=0) * (1.0 / width)
        for k in range(1, head_count):
            part_copy(k, step).wait()
        grad = parts[head, rows, :].astype(F32)
        for k in range(1, head_count):
            grad = grad + arrived[k - 1, rows, :].astype(F32)
        cubed = inv_rms * inv_rms * inv_rms
        out_ref[rows, :] = (
            d_ref[rows, :].astype(F32)
            + inv_rms * gain_mine_ref[...] * grad
            - mine_ref[rows, :].astype(F32) * (cubed * term)
        ).astype(BF16)
        return carry

    lax.fori_loop(0, chunks, final_step, 0)


def whole(shape):
    return pl.BlockSpec(shape, lambda i, *refs: (0,) * len(shape))


def run(kernel, scalars, args, outs, scratch=(), **params):
    return pl.pallas_call(
        kernel,
        out_shape=outs,
        grid_spec=pltpu.PrefetchScalarGridSpec(
            num_scalar_prefetch=len(scalars),
            grid=(1,),
            in_specs=[whole(value.shape) for value in args],
            out_specs=jax.tree.map(lambda out: whole(out.shape), outs),
            scratch_shapes=list(scratch),
        ),
        compiler_params=pltpu.CompilerParams(vmem_limit_bytes=VMEM_LIMIT, **params),
    )(*scalars, *args)


def shards(node_features, gain, w_qkv, d_out, pattern, counts):
    seq_count = lax.axis_size("seq")
    my_index = lax.axis_index("seq")
    row_count, width = node_features.shape
    block_count = row_count // BLOCK
    col_count = w_qkv.shape[2]
    head_count = width // col_count
    slot_count = block_count * EXPD
    capacity = max(2, 3 * slot_count // (2 * seq_count))
    slots_all = seq_count * capacity
    kv_width = 2 * col_count
    col_start = lax.axis_index("head") * col_count
    gain_row = gain.reshape(1, width)
    x_mine, d_mine, gain_mine = (
        lax.dynamic_slice_in_dim(value, col_start, col_count, 1)
        for value in (node_features, d_out, gain_row)
    )
    shape = jax.ShapeDtypeStruct

    owners = (pattern // block_count).reshape(seq_count, slot_count)
    in_owner = (pattern % block_count).reshape(seq_count, slot_count)
    before = jnp.arange(slot_count)[:, None] > jnp.arange(slot_count)[None, :]
    same = owners[:, :, None] == owners[:, None, :]
    ranks = jnp.sum((same & before[None]).astype(jnp.int32), axis=2)
    places = jnp.arange(capacity, dtype=jnp.int32)
    picked = (owners[:, None, :] == my_index) & (ranks[:, None, :] == places[None, :, None])
    sent_from = jnp.sum(jnp.where(picked, in_owner[:, None, :], 0), axis=2).reshape(-1)
    filled = jnp.any(picked, axis=2).astype(jnp.int32).reshape(-1)
    my_slots = lax.dynamic_index_in_dim(owners * capacity + ranks, my_index, 0, keepdims=False)

    normed, queries, kv_local, outgoing = run(
        project_kernel,
        (sent_from,),
        (node_features, gain_row, w_qkv),
        (
            shape((row_count, width), BF16),
            shape((row_count, col_count), BF16),
            shape((block_count, BLOCK, kv_width), BF16),
            shape((slots_all, BLOCK, kv_width), BF16),
        ),
        scratch=(pltpu.VMEM((width, 3 * col_count), BF16),),
    )
    incoming = lax.all_to_all(outgoing, "seq", split_axis=0, concat_axis=0, tiled=True)
    layer_output, grad_queries, own, returning = run(
        attend_kernel,
        (my_slots, counts),
        (queries, kv_local, incoming, x_mine, d_mine),
        (
            shape((row_count, col_count), BF16),
            shape((row_count, col_count), BF16),
            shape((block_count, BLOCK, kv_width), F32),
            shape((slots_all, BLOCK, kv_width), BF16),
        ),
    )
    returned = lax.all_to_all(returning, "seq", split_axis=0, concat_axis=0, tiled=True)
    share = width // seq_count
    grads, weight_parts = run(
        functools.partial(gather_kernel, node_count=row_count * seq_count),
        (sent_from, filled),
        (own, returned, grad_queries, normed),
        (
            shape((row_count, 3 * col_count), BF16),
            shape((seq_count, 3, share, col_count), BF16),
        ),
        scratch=(
            pltpu.VMEM((block_count, BLOCK, kv_width), F32),
            pltpu.VMEM((width, 3 * col_count), F32),
        ),
    )
    others = head_count - 1
    chunks = row_count // CHUNK
    dma = pltpu.SemaphoreType.DMA
    grad_input, grad_weights = run(
        exchange_kernel,
        (),
        (grads, weight_parts, node_features, x_mine, d_mine, gain_row, gain_mine, w_qkv),
        (
            shape((row_count, col_count), BF16),
            shape((3, share, col_count), F32),
        ),
        scratch=(
            pltpu.VMEM((width, 3 * col_count), BF16),
            pltpu.VMEM((head_count, row_count, col_count), BF16),
            pltpu.VMEM((others, row_count, col_count), BF16),
            pltpu.VMEM((block_count, 8, BLOCK), F32),
            pltpu.VMEM((others, block_count, 8, BLOCK), F32),
            pltpu.VMEM((seq_count - 1, 3, share, col_count), BF16),
            dma((others, chunks)),
            dma((others, chunks)),
            dma((others,)),
            dma((others,)),
            dma((seq_count - 1,)),
            dma((seq_count - 1,)),
        ),
        collective_id=0,
        has_side_effects=True,
    )
    return (layer_output, grad_input, grad_weights)


def solution(mesh):
    in_specs = (P("seq", None), P(), P(None, None, "head"), P("seq", None), P(), P("seq"))
    out_specs = (P("seq", "head"), P("seq", "head"), P(None, "seq", "head"))
    return jax.shard_map(shards, mesh=mesh, in_specs=in_specs, out_specs=out_specs, check_vma=False)
```

```python
import functools
import math

import jax
import jax.numpy as jnp
from jax import lax
from jax.experimental import pallas as pl
from jax.experimental.pallas import tpu as pltpu
from jax.sharding import PartitionSpec as P

HEAD_DIM = 64
BLOCK = 128
EXPD = 3
CHUNK = 256


EPS = 1e-06
F32 = jnp.float32
BF16 = jnp.bfloat16
VMEM_LIMIT = 50 * 1024 * 1024

CONTRACT_COLS = (((1,), (1,)), ((), ()))
CONTRACT_ROWS = (((0,), (0,)), ((), ()))


def rows_of(index, size):
    return pl.ds(pl.multiple_of(index * size, size), size)


def join_weights(w_ref, joined, cols):
    for member in range(3):
        joined[:, member * cols : (member + 1) * cols] = w_ref[member]


def project_kernel(
    sent_from,
    x_ref,
    gain_ref,
    w_ref,
    normed_ref,
    q_ref,
    kv_ref,
    in_ref,
    joined,
    relayed,
    near,
    far,
    relay_send,
    relay_recv,
    near_send,
    near_recv,
    far_send,
    far_recv,
    local_sem,
):
    cols = w_ref.shape[2]
    per_chunk = CHUNK // BLOCK
    seq_count, capacity = in_ref.shape[:2]
    half = seq_count // 2
    seq = lax.axis_index("seq")
    across = lax.rem(seq + half, seq_count)
    base = (seq // half) * half
    mesh_type = pl.DeviceIdType.MESH

    def mate(k):
        return base + lax.rem(seq - base + k, half)

    barrier = pltpu.get_barrier_semaphore()
    pl.semaphore_signal(barrier, inc=1, device_id={"seq": across}, device_id_type=mesh_type)
    for k in range(1, half):
        pl.semaphore_signal(barrier, inc=1, device_id={"seq": mate(k)}, device_id_type=mesh_type)

    join_weights(w_ref, joined, cols)

    def project(step, carry):
        rows = rows_of(step, CHUNK)
        x = x_ref[rows, :].astype(F32)
        inv_rms = lax.rsqrt(jnp.mean(x * x, axis=1, keepdims=True) + EPS)
        normed = (x * inv_rms * gain_ref[...]).astype(BF16)
        normed_ref[rows, :] = normed
        made = jnp.dot(normed, joined[...], preferred_element_type=F32).astype(BF16)
        q_ref[rows, :] = made[:, :cols]
        kv_ref[pl.ds(step * per_chunk, per_chunk)] = made[:, cols:].reshape(
            per_chunk, BLOCK, 2 * cols
        )
        return carry

    lax.fori_loop(0, x_ref.shape[0] // CHUNK, project, 0)
    pl.semaphore_wait(barrier, half)

    relay = pltpu.make_async_remote_copy(
        src_ref=kv_ref,
        dst_ref=relayed,
        send_sem=relay_send,
        recv_sem=relay_recv,
        device_id={"seq": across},
        device_id_type=mesh_type,
    )
    relay.start()

    def deal(source, which, owner, stage, send, recv):
        sends = []
        for k in list(range(1, half)) + [0]:
            for rank in range(capacity):
                place = sent_from[(which * seq_count + mate(k)) * capacity + rank]
                stage[k, rank] = source[place]
            if k:
                copy = pltpu.make_async_remote_copy(
                    src_ref=stage.at[k],
                    dst_ref=in_ref.at[owner],
                    send_sem=send.at[k - 1],
                    recv_sem=recv.at[k - 1],
                    device_id={"seq": mate(k)},
                    device_id_type=mesh_type,
                )
            else:
                copy = pltpu.make_async_copy(stage.at[0], in_ref.at[owner], local_sem.at[which])
            copy.start()
            sends.append(copy)
        return sends

    sends = deal(kv_ref, 0, seq, near, near_send, near_recv)
    relay.wait()
    sends += deal(relayed, 1, across, far, far_send, far_recv)
    for copy in sends:
        copy.wait()


def attend_kernel(
    slots, counts, q_ref, kv_ref, slot_ref, x_ref, d_ref, layer_ref, gq_ref, own_ref, back_ref
):
    cols = q_ref.shape[1]
    heads_here = cols // HEAD_DIM
    scale = 1.0 / math.sqrt(HEAD_DIM)
    keys_all = (1 + EXPD) * BLOCK
    lane_head = lax.broadcasted_iota(jnp.int32, (BLOCK, cols), 1) // HEAD_DIM
    key_place = lax.broadcasted_iota(jnp.int32, (1, keys_all), 1)

    def spread(value):
        return jnp.concatenate(
            [jnp.where(lane_head == h, value, jnp.zeros_like(value)) for h in range(heads_here)],
            axis=0,
        )

    def merge(value):
        made = value[:BLOCK]
        for h in range(1, heads_here):
            made = jnp.where(lane_head == h, value[h * BLOCK : (h + 1) * BLOCK], made)
        return made

    def block_step(block, carry):
        rows = rows_of(block, BLOCK)
        places = [slots[block * EXPD + j] for j in range(EXPD)]
        own = kv_ref[block]
        listed = jnp.concatenate([own] + [slot_ref[place] for place in places], axis=0)
        keys = listed[:, :cols]
        values = listed[:, cols:]
        queries = spread(q_ref[rows, :])
        grads = spread(d_ref[rows, :])
        scores = lax.dot_general(queries, keys, CONTRACT_COLS, preferred_element_type=F32) * scale
        scores = jnp.where(key_place < (counts[block] + 1) * BLOCK, scores, -jnp.inf)
        powers = jnp.exp(scores - jnp.max(scores, axis=1, keepdims=True))
        attention = powers * (1.0 / jnp.sum(powers, axis=1, keepdims=True))
        low = attention.astype(BF16)
        attended = jnp.dot(low, values, preferred_element_type=F32)
        layer_ref[rows, :] = (x_ref[rows, :].astype(F32) + merge(attended)).astype(BF16)
        grad_attention = lax.dot_general(grads, values, CONTRACT_COLS, preferred_element_type=F32)
        row_dot = jnp.sum(grads.astype(F32) * attended, axis=1, keepdims=True)
        grad_scores = (attention * (grad_attention - row_dot) * scale).astype(BF16)
        gq_ref[rows, :] = merge(jnp.dot(grad_scores, keys, preferred_element_type=F32)).astype(BF16)
        grad_keys = lax.dot_general(grad_scores, queries, CONTRACT_ROWS, preferred_element_type=F32)
        grad_values = lax.dot_general(low, grads, CONTRACT_ROWS, preferred_element_type=F32)
        own_ref[block] = jnp.concatenate([grad_keys[:BLOCK], grad_values[:BLOCK]], axis=1)
        for j, place in enumerate(places):
            part = slice((j + 1) * BLOCK, (j + 2) * BLOCK)
            back_ref[place] = jnp.concatenate([grad_keys[part], grad_values[part]], axis=1).astype(
                BF16
            )
        return carry

    lax.fori_loop(0, kv_ref.shape[0], block_step, 0)


def gather_kernel(
    sent_from, filled, own_ref, back_ref, gq_ref, normed_ref, grads_ref, gw_ref, total, sums, *, node_count
):
    cols = gq_ref.shape[1]
    width = normed_ref.shape[1]
    per_chunk = CHUNK // BLOCK
    sums[...] = jnp.zeros_like(sums)
    total[...] = own_ref[...]

    def gather(slot, carry):
        @pl.when(filled[slot] > 0)
        def _():
            place = sent_from[slot]
            total[place] = total[place] + back_ref[slot].astype(F32)

        return carry

    lax.fori_loop(0, back_ref.shape[0], gather, 0)

    def chunk_step(step, carry):
        rows = rows_of(step, CHUNK)
        grad_kv = total[pl.ds(step * per_chunk, per_chunk)].reshape(CHUNK, 2 * cols).astype(BF16)
        grads = jnp.concatenate([gq_ref[rows, :], grad_kv], axis=1)
        grads_ref[rows, :] = grads
        sums[...] += lax.dot_general(
            normed_ref[rows, :], grads, CONTRACT_ROWS, preferred_element_type=F32
        )
        return carry

    lax.fori_loop(0, gq_ref.shape[0] // CHUNK, chunk_step, 0)
    seq_count = gw_ref.shape[0]
    share = width // seq_count
    factor = 1.0 / math.sqrt(node_count)
    for peer in range(seq_count):
        for member in range(3):
            gw_ref[peer, member] = (
                sums[peer * share : (peer + 1) * share, member * cols : (member + 1) * cols]
                * factor
            ).astype(BF16)


def exchange_kernel(
    grads_ref,
    gw_ref,
    x_ref,
    mine_ref,
    d_ref,
    gain_ref,
    gain_mine_ref,
    w_ref,
    out_ref,
    weights_ref,
    joined,
    parts,
    arrived,
    terms,
    terms_in,
    gw_in,
    part_send,
    part_recv,
    term_send,
    term_recv,
    gw_send,
    gw_recv,
):
    cols = w_ref.shape[2]
    row_count, width = x_ref.shape
    head_count = parts.shape[0]
    seq_count = gw_ref.shape[0]
    per_chunk = CHUNK // BLOCK
    chunks = row_count // CHUNK
    head = lax.axis_index("head")
    seq = lax.axis_index("seq")
    mesh_type = pl.DeviceIdType.MESH

    def head_peer(k):
        return lax.rem(head + k, head_count)

    def seq_peer(k):
        return lax.rem(seq + k, seq_count)

    barrier = pltpu.get_barrier_semaphore()
    for k in range(1, head_count):
        pl.semaphore_signal(
            barrier, inc=1, device_id={"head": head_peer(k)}, device_id_type=mesh_type
        )
    for k in range(1, seq_count):
        pl.semaphore_signal(
            barrier, inc=1, device_id={"seq": seq_peer(k)}, device_id_type=mesh_type
        )
    pl.semaphore_wait(barrier, head_count + seq_count - 2)

    def weight_copy(k):
        return pltpu.make_async_remote_copy(
            src_ref=gw_ref.at[seq_peer(k)],
            dst_ref=gw_in.at[k - 1],
            send_sem=gw_send.at[k - 1],
            recv_sem=gw_recv.at[k - 1],
            device_id={"seq": seq_peer(k)},
            device_id_type=mesh_type,
        )

    def part_copy(k, step):
        rows = rows_of(step, CHUNK)
        return pltpu.make_async_remote_copy(
            src_ref=parts.at[head_peer(k), rows],
            dst_ref=arrived.at[k - 1, rows],
            send_sem=part_send.at[k - 1, step],
            recv_sem=part_recv.at[k - 1, step],
            device_id={"head": head_peer(k)},
            device_id_type=mesh_type,
        )

    def term_copy(k):
        return pltpu.make_async_remote_copy(
            src_ref=terms,
            dst_ref=terms_in.at[k - 1],
            send_sem=term_send.at[k - 1],
            recv_sem=term_recv.at[k - 1],
            device_id={"head": head_peer(k)},
            device_id_type=mesh_type,
        )

    for k in range(1, seq_count):
        weight_copy(k).start()
    join_weights(w_ref, joined, cols)

    def chunk_step(step, carry):
        rows = rows_of(step, CHUNK)
        grad_normed = lax.dot_general(
            grads_ref[rows, :], joined[...], CONTRACT_COLS, preferred_element_type=F32
        )
        for part in range(head_count):
            parts[part, rows, :] = grad_normed[:, part * cols : (part + 1) * cols].astype(BF16)
        for k in range(1, head_count):
            part_copy(k, step).start()
        term = jnp.sum(
            x_ref[rows, :].astype(F32) * gain_ref[...] * grad_normed, axis=1, keepdims=True
        )
        for inner in range(per_chunk):
            piece = jnp.broadcast_to(term[inner * BLOCK : (inner + 1) * BLOCK], (BLOCK, BLOCK))
            terms[step * per_chunk + inner] = piece.T[:8]
        return carry

    lax.fori_loop(0, chunks, chunk_step, 0)
    for k in range(1, head_count):
        term_copy(k).start()
    for k in range(1, seq_count):
        weight_copy(k).wait()
    total = gw_ref[seq].astype(F32)
    for k in range(1, seq_count):
        total = total + gw_in[k - 1].astype(F32)
    weights_ref[...] = total
    for k in range(1, head_count):
        term_copy(k).wait()

    def final_step(step, carry):
        rows = rows_of(step, CHUNK)
        x = x_ref[rows, :].astype(F32)
        inv_rms = lax.rsqrt(jnp.mean(x * x, axis=1, keepdims=True) + EPS)
        columns = []
        for inner in range(per_chunk):
            row = terms[step * per_chunk + inner]
            for k in range(1, head_count):
                row = row + terms_in[k - 1, step * per_chunk + inner]
            columns.append(jnp.broadcast_to(row[:1], (BLOCK, BLOCK)).T[:, :1])
        term = jnp.concatenate(columns, axis=0) * (1.0 / width)
        for k in range(1, head_count):
            part_copy(k, step).wait()
        grad = parts[head, rows, :].astype(F32)
        for k in range(1, head_count):
            grad = grad + arrived[k - 1, rows, :].astype(F32)
        cubed = inv_rms * inv_rms * inv_rms
        out_ref[rows, :] = (
            d_ref[rows, :].astype(F32)
            + inv_rms * gain_mine_ref[...] * grad
            - mine_ref[rows, :].astype(F32) * (cubed * term)
        ).astype(BF16)
        return carry

    lax.fori_loop(0, chunks, final_step, 0)


def whole(shape):
    return pl.BlockSpec(shape, lambda i, *refs: (0,) * len(shape))


def run(kernel, scalars, args, outs, scratch=(), **params):
    return pl.pallas_call(
        kernel,
        out_shape=outs,
        grid_spec=pltpu.PrefetchScalarGridSpec(
            num_scalar_prefetch=len(scalars),
            grid=(1,),
            in_specs=[whole(value.shape) for value in args],
            out_specs=jax.tree.map(lambda out: whole(out.shape), outs),
            scratch_shapes=list(scratch),
        ),
        compiler_params=pltpu.CompilerParams(vmem_limit_bytes=VMEM_LIMIT, **params),
    )(*scalars, *args)


def shards(node_features, gain, w_qkv, d_out, pattern, counts):
    seq_count = lax.axis_size("seq")
    my_index = lax.axis_index("seq")
    row_count, width = node_features.shape
    block_count = row_count // BLOCK
    col_count = w_qkv.shape[2]
    head_count = width // col_count
    slot_count = block_count * EXPD
    capacity = max(2, 3 * slot_count // (2 * seq_count))
    slots_all = seq_count * capacity
    kv_width = 2 * col_count
    col_start = lax.axis_index("head") * col_count
    gain_row = gain.reshape(1, width)
    x_mine, d_mine, gain_mine = (
        lax.dynamic_slice_in_dim(value, col_start, col_count, 1)
        for value in (node_features, d_out, gain_row)
    )
    shape = jax.ShapeDtypeStruct

    owners = (pattern // block_count).reshape(seq_count, slot_count)
    in_owner = (pattern % block_count).reshape(seq_count, slot_count)
    before = jnp.arange(slot_count)[:, None] > jnp.arange(slot_count)[None, :]
    same = owners[:, :, None] == owners[:, None, :]
    ranks = jnp.sum((same & before[None]).astype(jnp.int32), axis=2)
    places = jnp.arange(capacity, dtype=jnp.int32)
    half = seq_count // 2
    holders = jnp.stack([my_index, (my_index + half) % seq_count]).astype(jnp.int32)
    picked = (owners[None, :, None, :] == holders[:, None, None, None]) & (
        ranks[None, :, None, :] == places[None, None, :, None]
    )
    dealt = jnp.sum(jnp.where(picked, in_owner[None, :, None, :], 0), axis=3)
    sent_from = dealt[0].reshape(-1)
    filled = jnp.any(picked[0], axis=2).astype(jnp.int32).reshape(-1)
    my_slots = lax.dynamic_index_in_dim(owners * capacity + ranks, my_index, 0, keepdims=False)

    dma = pltpu.SemaphoreType.DMA
    vmem = pl.BlockSpec(memory_space=pltpu.VMEM)
    normed, queries, kv_local, incoming = pl.pallas_call(
        project_kernel,
        out_shape=(
            shape((row_count, width), BF16),
            shape((row_count, col_count), BF16),
            shape((block_count, BLOCK, kv_width), BF16),
            shape((seq_count, capacity, BLOCK, kv_width), BF16),
        ),
        in_specs=[pl.BlockSpec(memory_space=pltpu.SMEM), vmem, vmem, vmem],
        out_specs=(vmem, vmem, vmem, pl.BlockSpec(memory_space=pl.ANY)),
        scratch_shapes=[
            pltpu.VMEM((width, 3 * col_count), BF16),
            pltpu.VMEM((block_count, BLOCK, kv_width), BF16),
            pltpu.VMEM((half, capacity, BLOCK, kv_width), BF16),
            pltpu.VMEM((half, capacity, BLOCK, kv_width), BF16),
            dma,
            dma,
            dma((half - 1,)),
            dma((half - 1,)),
            dma((half - 1,)),
            dma((half - 1,)),
            dma((2,)),
        ],
        compiler_params=pltpu.CompilerParams(
            vmem_limit_bytes=VMEM_LIMIT, collective_id=1, has_side_effects=True
        ),
    )(dealt.reshape(-1), node_features, gain_row, w_qkv)
    incoming = incoming.reshape(slots_all, BLOCK, kv_width)
    layer_output, grad_queries, own, returning = run(
        attend_kernel,
        (my_slots, counts),
        (queries, kv_local, incoming, x_mine, d_mine),
        (
            shape((row_count, col_count), BF16),
            shape((row_count, col_count), BF16),
            shape((block_count, BLOCK, kv_width), F32),
            shape((slots_all, BLOCK, kv_width), BF16),
        ),
    )
    returned = lax.all_to_all(returning, "seq", split_axis=0, concat_axis=0, tiled=True)
    share = width // seq_count
    grads, weight_parts = run(
        functools.partial(gather_kernel, node_count=row_count * seq_count),
        (sent_from, filled),
        (own, returned, grad_queries, normed),
        (
            shape((row_count, 3 * col_count), BF16),
            shape((seq_count, 3, share, col_count), BF16),
        ),
        scratch=(
            pltpu.VMEM((block_count, BLOCK, kv_width), F32),
            pltpu.VMEM((width, 3 * col_count), F32),
        ),
    )
    others = head_count - 1
    chunks = row_count // CHUNK
    grad_input, grad_weights = run(
        exchange_kernel,
        (),
        (grads, weight_parts, node_features, x_mine, d_mine, gain_row, gain_mine, w_qkv),
        (
            shape((row_count, col_count), BF16),
            shape((3, share, col_count), F32),
        ),
        scratch=(
            pltpu.VMEM((width, 3 * col_count), BF16),
            pltpu.VMEM((head_count, row_count, col_count), BF16),
            pltpu.VMEM((others, row_count, col_count), BF16),
            pltpu.VMEM((block_count, 8, BLOCK), F32),
            pltpu.VMEM((others, block_count, 8, BLOCK), F32),
            pltpu.VMEM((seq_count - 1, 3, share, col_count), BF16),
            dma((others, chunks)),
            dma((others, chunks)),
            dma((others,)),
            dma((others,)),
            dma((seq_count - 1,)),
            dma((seq_count - 1,)),
        ),
        collective_id=0,
        has_side_effects=True,
    )
    return (layer_output, grad_input, grad_weights)


def solution(mesh):
    in_specs = (P("seq", None), P(), P(None, None, "head"), P("seq", None), P(), P("seq"))
    out_specs = (P("seq", "head"), P("seq", "head"), P(None, "seq", "head"))
    return jax.shard_map(shards, mesh=mesh, in_specs=in_specs, out_specs=out_specs, check_vma=False)
```

```python
import functools
import math

import jax
import jax.numpy as jnp
from jax import lax
from jax.experimental import pallas as pl
from jax.experimental.pallas import tpu as pltpu
from jax.sharding import PartitionSpec as P

HEAD_DIM = 64
BLOCK = 128
EXPD = 3
CHUNK = 256


EPS = 1e-06
F32 = jnp.float32
BF16 = jnp.bfloat16
VMEM_LIMIT = 50 * 1024 * 1024

CONTRACT_COLS = (((1,), (1,)), ((), ()))
CONTRACT_ROWS = (((0,), (0,)), ((), ()))


def rows_of(index, size):
    return pl.ds(pl.multiple_of(index * size, size), size)


def join_weights(w_ref, joined, cols):
    for member in range(3):
        joined[:, member * cols : (member + 1) * cols] = w_ref[member]


def project_kernel(
    sent_from,
    x_ref,
    gain_ref,
    w_ref,
    normed_ref,
    q_ref,
    kv_ref,
    in_ref,
    joined,
    relayed,
    near,
    far,
    relay_send,
    relay_recv,
    near_send,
    near_recv,
    far_send,
    far_recv,
    local_sem,
):
    cols = w_ref.shape[2]
    per_chunk = CHUNK // BLOCK
    seq_count, capacity = in_ref.shape[:2]
    half = seq_count // 2
    seq = lax.axis_index("seq")
    across = lax.rem(seq + half, seq_count)
    base = (seq // half) * half
    mesh_type = pl.DeviceIdType.MESH

    def mate(k):
        return base + lax.rem(seq - base + k, half)

    barrier = pltpu.get_barrier_semaphore()
    pl.semaphore_signal(barrier, inc=1, device_id={"seq": across}, device_id_type=mesh_type)
    for k in range(1, half):
        pl.semaphore_signal(barrier, inc=1, device_id={"seq": mate(k)}, device_id_type=mesh_type)

    join_weights(w_ref, joined, cols)

    def project(step, carry):
        rows = rows_of(step, CHUNK)
        x = x_ref[rows, :].astype(F32)
        inv_rms = lax.rsqrt(jnp.mean(x * x, axis=1, keepdims=True) + EPS)
        normed = (x * inv_rms * gain_ref[...]).astype(BF16)
        normed_ref[rows, :] = normed
        made = jnp.dot(normed, joined[...], preferred_element_type=F32).astype(BF16)
        q_ref[rows, :] = made[:, :cols]
        kv_ref[pl.ds(step * per_chunk, per_chunk)] = made[:, cols:].reshape(
            per_chunk, BLOCK, 2 * cols
        )
        return carry

    lax.fori_loop(0, x_ref.shape[0] // CHUNK, project, 0)
    pl.semaphore_wait(barrier, half)

    relay = pltpu.make_async_remote_copy(
        src_ref=kv_ref,
        dst_ref=relayed,
        send_sem=relay_send,
        recv_sem=relay_recv,
        device_id={"seq": across},
        device_id_type=mesh_type,
    )
    relay.start()

    def deal(source, which, owner, stage, send, recv):
        sends = []
        for k in list(range(1, half)) + [0]:
            for rank in range(capacity):
                place = sent_from[(which * seq_count + mate(k)) * capacity + rank]
                stage[k, rank] = source[place]
            if k:
                copy = pltpu.make_async_remote_copy(
                    src_ref=stage.at[k],
                    dst_ref=in_ref.at[owner],
                    send_sem=send.at[k - 1],
                    recv_sem=recv.at[k - 1],
                    device_id={"seq": mate(k)},
                    device_id_type=mesh_type,
                )
            else:
                copy = pltpu.make_async_copy(stage.at[0], in_ref.at[owner], local_sem.at[which])
            copy.start()
            sends.append(copy)
        return sends

    sends = deal(kv_ref, 0, seq, near, near_send, near_recv)
    relay.wait()
    sends += deal(relayed, 1, across, far, far_send, far_recv)
    for copy in sends:
        copy.wait()


def attend_kernel(
    slots, counts, q_ref, kv_ref, slot_ref, x_ref, d_ref, layer_ref, gq_ref, own_ref, back_ref
):
    cols = q_ref.shape[1]
    heads_here = cols // HEAD_DIM
    scale = 1.0 / math.sqrt(HEAD_DIM)
    keys_all = (1 + EXPD) * BLOCK
    lane_head = lax.broadcasted_iota(jnp.int32, (BLOCK, cols), 1) // HEAD_DIM
    key_place = lax.broadcasted_iota(jnp.int32, (1, keys_all), 1)

    def spread(value):
        return jnp.concatenate(
            [jnp.where(lane_head == h, value, jnp.zeros_like(value)) for h in range(heads_here)],
            axis=0,
        )

    def merge(value):
        made = value[:BLOCK]
        for h in range(1, heads_here):
            made = jnp.where(lane_head == h, value[h * BLOCK : (h + 1) * BLOCK], made)
        return made

    def block_step(block, carry):
        rows = rows_of(block, BLOCK)
        places = [slots[block * EXPD + j] for j in range(EXPD)]
        own = kv_ref[block]
        listed = jnp.concatenate([own] + [slot_ref[place] for place in places], axis=0)
        keys = listed[:, :cols]
        values = listed[:, cols:]
        queries = spread(q_ref[rows, :])
        grads = spread(d_ref[rows, :])
        scores = lax.dot_general(queries, keys, CONTRACT_COLS, preferred_element_type=F32) * scale
        scores = jnp.where(key_place < (counts[block] + 1) * BLOCK, scores, -jnp.inf)
        powers = jnp.exp(scores - jnp.max(scores, axis=1, keepdims=True))
        attention = powers * (1.0 / jnp.sum(powers, axis=1, keepdims=True))
        low = attention.astype(BF16)
        attended = jnp.dot(low, values, preferred_element_type=F32)
        layer_ref[rows, :] = (x_ref[rows, :].astype(F32) + merge(attended)).astype(BF16)
        grad_attention = lax.dot_general(grads, values, CONTRACT_COLS, preferred_element_type=F32)
        row_dot = jnp.sum(grads.astype(F32) * attended, axis=1, keepdims=True)
        grad_scores = (attention * (grad_attention - row_dot) * scale).astype(BF16)
        gq_ref[rows, :] = merge(jnp.dot(grad_scores, keys, preferred_element_type=F32)).astype(BF16)
        grad_keys = lax.dot_general(grad_scores, queries, CONTRACT_ROWS, preferred_element_type=F32)
        grad_values = lax.dot_general(low, grads, CONTRACT_ROWS, preferred_element_type=F32)
        own_ref[block] = jnp.concatenate([grad_keys[:BLOCK], grad_values[:BLOCK]], axis=1)
        for j, place in enumerate(places):
            part = slice((j + 1) * BLOCK, (j + 2) * BLOCK)
            back_ref[place] = jnp.concatenate([grad_keys[part], grad_values[part]], axis=1).astype(
                BF16
            )
        return carry

    lax.fori_loop(0, kv_ref.shape[0], block_step, 0)


def return_kernel(
    far_from,
    back_ref,
    near_ref,
    relay_ref,
    far_in,
    summed,
    far_send,
    far_recv,
    near_send,
    near_recv,
    relay_send,
    relay_recv,
    local_sem,
):
    seq_count, capacity = back_ref.shape[:2]
    block_count = relay_ref.shape[0]
    half = seq_count // 2
    piece = BLOCK // 2
    seq = lax.axis_index("seq")
    across = lax.rem(seq + half, seq_count)
    base = (seq // half) * half
    mesh_type = pl.DeviceIdType.MESH

    def mate(k):
        return base + lax.rem(seq - base + k, half)

    barrier = pltpu.get_barrier_semaphore()
    pl.semaphore_signal(barrier, inc=1, device_id={"seq": across}, device_id_type=mesh_type)
    for k in range(1, half):
        pl.semaphore_signal(barrier, inc=1, device_id={"seq": mate(k)}, device_id_type=mesh_type)
    pl.semaphore_wait(barrier, half)

    fars = []
    nears = []
    for k in range(1, half):
        fars.append(
            pltpu.make_async_remote_copy(
                src_ref=back_ref.at[lax.rem(mate(k) + half, seq_count)],
                dst_ref=far_in.at[k - 1],
                send_sem=far_send.at[k - 1],
                recv_sem=far_recv.at[k - 1],
                device_id={"seq": mate(k)},
                device_id_type=mesh_type,
            )
        )
        nears.append(
            pltpu.make_async_remote_copy(
                src_ref=back_ref.at[mate(k)],
                dst_ref=near_ref.at[k],
                send_sem=near_send.at[k - 1],
                recv_sem=near_recv.at[k - 1],
                device_id={"seq": mate(k)},
                device_id_type=mesh_type,
            )
        )
    nears.append(pltpu.make_async_copy(back_ref.at[seq], near_ref.at[0], local_sem))
    for copy in fars:
        copy.start()
    for copy in fars:
        copy.wait()
    for copy in nears:
        copy.start()

    def add_block(block, carry):
        for part in range(2):
            rows = slice(part * piece, (part + 1) * piece)
            made = jnp.zeros((piece, back_ref.shape[3]), F32)
            for k in range(half):
                for rank in range(capacity):
                    if k:
                        term = far_in[k - 1, rank, rows, :]
                    else:
                        term = back_ref[across, rank, rows, :]
                    listed = far_from[k * capacity + rank] == block
                    made = made + jnp.where(listed, term.astype(F32), 0.0)
            summed[block, rows, :] = made.astype(BF16)
        return carry

    lax.fori_loop(0, block_count, add_block, 0)
    relay = pltpu.make_async_remote_copy(
        src_ref=summed,
        dst_ref=relay_ref,
        send_sem=relay_send,
        recv_sem=relay_recv,
        device_id={"seq": across},
        device_id_type=mesh_type,
    )
    relay.start()
    for copy in nears:
        copy.wait()
    relay.wait()


def gather_kernel(
    near_from,
    own_ref,
    near_ref,
    relay_ref,
    gq_ref,
    normed_ref,
    grads_ref,
    gw_ref,
    total,
    sums,
    *,
    node_count,
):
    cols = gq_ref.shape[1]
    width = normed_ref.shape[1]
    per_chunk = CHUNK // BLOCK
    sums[...] = jnp.zeros_like(sums)
    total[...] = own_ref[...] + relay_ref[...].astype(F32)

    def gather(slot, carry):
        place = near_from[slot]

        @pl.when(place >= 0)
        def _():
            total[place] = total[place] + near_ref[slot].astype(F32)

        return carry

    lax.fori_loop(0, near_ref.shape[0], gather, 0)

    def chunk_step(step, carry):
        rows = rows_of(step, CHUNK)
        grad_kv = total[pl.ds(step * per_chunk, per_chunk)].reshape(CHUNK, 2 * cols).astype(BF16)
        grads = jnp.concatenate([gq_ref[rows, :], grad_kv], axis=1)
        grads_ref[rows, :] = grads
        sums[...] += lax.dot_general(
            normed_ref[rows, :], grads, CONTRACT_ROWS, preferred_element_type=F32
        )
        return carry

    lax.fori_loop(0, gq_ref.shape[0] // CHUNK, chunk_step, 0)
    seq_count = gw_ref.shape[0]
    share = width // seq_count
    factor = 1.0 / math.sqrt(node_count)
    for peer in range(seq_count):
        for member in range(3):
            gw_ref[peer, member] = (
                sums[peer * share : (peer + 1) * share, member * cols : (member + 1) * cols]
                * factor
            ).astype(BF16)


def exchange_kernel(
    grads_ref,
    gw_ref,
    x_ref,
    mine_ref,
    d_ref,
    gain_ref,
    gain_mine_ref,
    w_ref,
    out_ref,
    weights_ref,
    joined,
    parts,
    arrived,
    terms,
    terms_in,
    gw_in,
    part_send,
    part_recv,
    term_send,
    term_recv,
    gw_send,
    gw_recv,
):
    cols = w_ref.shape[2]
    row_count, width = x_ref.shape
    head_count = parts.shape[0]
    seq_count = gw_ref.shape[0]
    per_chunk = CHUNK // BLOCK
    chunks = row_count // CHUNK
    head = lax.axis_index("head")
    seq = lax.axis_index("seq")
    mesh_type = pl.DeviceIdType.MESH

    def head_peer(k):
        return lax.rem(head + k, head_count)

    def seq_peer(k):
        return lax.rem(seq + k, seq_count)

    barrier = pltpu.get_barrier_semaphore()
    for k in range(1, head_count):
        pl.semaphore_signal(
            barrier, inc=1, device_id={"head": head_peer(k)}, device_id_type=mesh_type
        )
    for k in range(1, seq_count):
        pl.semaphore_signal(
            barrier, inc=1, device_id={"seq": seq_peer(k)}, device_id_type=mesh_type
        )
    pl.semaphore_wait(barrier, head_count + seq_count - 2)

    def weight_copy(k):
        return pltpu.make_async_remote_copy(
            src_ref=gw_ref.at[seq_peer(k)],
            dst_ref=gw_in.at[k - 1],
            send_sem=gw_send.at[k - 1],
            recv_sem=gw_recv.at[k - 1],
            device_id={"seq": seq_peer(k)},
            device_id_type=mesh_type,
        )

    def part_copy(k, step):
        rows = rows_of(step, CHUNK)
        return pltpu.make_async_remote_copy(
            src_ref=parts.at[head_peer(k), rows],
            dst_ref=arrived.at[k - 1, rows],
            send_sem=part_send.at[k - 1, step],
            recv_sem=part_recv.at[k - 1, step],
            device_id={"head": head_peer(k)},
            device_id_type=mesh_type,
        )

    def term_copy(k):
        return pltpu.make_async_remote_copy(
            src_ref=terms,
            dst_ref=terms_in.at[k - 1],
            send_sem=term_send.at[k - 1],
            recv_sem=term_recv.at[k - 1],
            device_id={"head": head_peer(k)},
            device_id_type=mesh_type,
        )

    for k in range(1, seq_count):
        weight_copy(k).start()
    join_weights(w_ref, joined, cols)

    def chunk_step(step, carry):
        rows = rows_of(step, CHUNK)
        grad_normed = lax.dot_general(
            grads_ref[rows, :], joined[...], CONTRACT_COLS, preferred_element_type=F32
        )
        for part in range(head_count):
            parts[part, rows, :] = grad_normed[:, part * cols : (part + 1) * cols].astype(BF16)
        for k in range(1, head_count):
            part_copy(k, step).start()
        term = jnp.sum(
            x_ref[rows, :].astype(F32) * gain_ref[...] * grad_normed, axis=1, keepdims=True
        )
        for inner in range(per_chunk):
            piece = jnp.broadcast_to(term[inner * BLOCK : (inner + 1) * BLOCK], (BLOCK, BLOCK))
            terms[step * per_chunk + inner] = piece.T[:8]
        return carry

    lax.fori_loop(0, chunks, chunk_step, 0)
    for k in range(1, head_count):
        term_copy(k).start()
    for k in range(1, seq_count):
        weight_copy(k).wait()
    total = gw_ref[seq].astype(F32)
    for k in range(1, seq_count):
        total = total + gw_in[k - 1].astype(F32)
    weights_ref[...] = total
    for k in range(1, head_count):
        term_copy(k).wait()

    def final_step(step, carry):
        rows = rows_of(step, CHUNK)
        x = x_ref[rows, :].astype(F32)
        inv_rms = lax.rsqrt(jnp.mean(x * x, axis=1, keepdims=True) + EPS)
        columns = []
        for inner in range(per_chunk):
            row = terms[step * per_chunk + inner]
            for k in range(1, head_count):
                row = row + terms_in[k - 1, step * per_chunk + inner]
            columns.append(jnp.broadcast_to(row[:1], (BLOCK, BLOCK)).T[:, :1])
        term = jnp.concatenate(columns, axis=0) * (1.0 / width)
        for k in range(1, head_count):
            part_copy(k, step).wait()
        grad = parts[head, rows, :].astype(F32)
        for k in range(1, head_count):
            grad = grad + arrived[k - 1, rows, :].astype(F32)
        cubed = inv_rms * inv_rms * inv_rms
        out_ref[rows, :] = (
            d_ref[rows, :].astype(F32)
            + inv_rms * gain_mine_ref[...] * grad
            - mine_ref[rows, :].astype(F32) * (cubed * term)
        ).astype(BF16)
        return carry

    lax.fori_loop(0, chunks, final_step, 0)


def whole(shape):
    return pl.BlockSpec(shape, lambda i, *refs: (0,) * len(shape))


def run(kernel, scalars, args, outs, scratch=(), **params):
    return pl.pallas_call(
        kernel,
        out_shape=outs,
        grid_spec=pltpu.PrefetchScalarGridSpec(
            num_scalar_prefetch=len(scalars),
            grid=(1,),
            in_specs=[whole(value.shape) for value in args],
            out_specs=jax.tree.map(lambda out: whole(out.shape), outs),
            scratch_shapes=list(scratch),
        ),
        compiler_params=pltpu.CompilerParams(vmem_limit_bytes=VMEM_LIMIT, **params),
    )(*scalars, *args)


def shards(node_features, gain, w_qkv, d_out, pattern, counts):
    seq_count = lax.axis_size("seq")
    my_index = lax.axis_index("seq")
    row_count, width = node_features.shape
    block_count = row_count // BLOCK
    col_count = w_qkv.shape[2]
    head_count = width // col_count
    slot_count = block_count * EXPD
    capacity = max(2, 3 * slot_count // (2 * seq_count))
    slots_all = seq_count * capacity
    kv_width = 2 * col_count
    col_start = lax.axis_index("head") * col_count
    gain_row = gain.reshape(1, width)
    x_mine, d_mine, gain_mine = (
        lax.dynamic_slice_in_dim(value, col_start, col_count, 1)
        for value in (node_features, d_out, gain_row)
    )
    shape = jax.ShapeDtypeStruct

    owners = (pattern // block_count).reshape(seq_count, slot_count)
    in_owner = (pattern % block_count).reshape(seq_count, slot_count)
    before = jnp.arange(slot_count)[:, None] > jnp.arange(slot_count)[None, :]
    same = owners[:, :, None] == owners[:, None, :]
    ranks = jnp.sum((same & before[None]).astype(jnp.int32), axis=2)
    places = jnp.arange(capacity, dtype=jnp.int32)
    peers = jnp.arange(seq_count, dtype=jnp.int32)
    half = seq_count // 2
    holders = jnp.stack([my_index, (my_index + half) % seq_count]).astype(jnp.int32)
    picked = (owners[None, :, None, :] == holders[:, None, None, None]) & (
        ranks[None, :, None, :] == places[None, None, :, None]
    )
    dealt = jnp.sum(jnp.where(picked, in_owner[None, :, None, :], 0), axis=3)
    taken = jnp.where(jnp.any(picked, axis=3), dealt, -1)
    base = (my_index // half) * half
    senders = base + (my_index - base - jnp.arange(half, dtype=jnp.int32)) % half
    near_from, far_from = (
        jnp.sum(
            jnp.where(
                senders[:, None, None] == peers[None, :, None], taken[which][None], 0
            ),
            axis=1,
        ).reshape(-1)
        for which in range(2)
    )
    my_slots = lax.dynamic_index_in_dim(owners * capacity + ranks, my_index, 0, keepdims=False)

    dma = pltpu.SemaphoreType.DMA
    vmem = pl.BlockSpec(memory_space=pltpu.VMEM)
    normed, queries, kv_local, incoming = pl.pallas_call(
        project_kernel,
        out_shape=(
            shape((row_count, width), BF16),
            shape((row_count, col_count), BF16),
            shape((block_count, BLOCK, kv_width), BF16),
            shape((seq_count, capacity, BLOCK, kv_width), BF16),
        ),
        in_specs=[pl.BlockSpec(memory_space=pltpu.SMEM), vmem, vmem, vmem],
        out_specs=(vmem, vmem, vmem, pl.BlockSpec(memory_space=pl.ANY)),
        scratch_shapes=[
            pltpu.VMEM((width, 3 * col_count), BF16),
            pltpu.VMEM((block_count, BLOCK, kv_width), BF16),
            pltpu.VMEM((half, capacity, BLOCK, kv_width), BF16),
            pltpu.VMEM((half, capacity, BLOCK, kv_width), BF16),
            dma,
            dma,
            dma((half - 1,)),
            dma((half - 1,)),
            dma((half - 1,)),
            dma((half - 1,)),
            dma((2,)),
        ],
        compiler_params=pltpu.CompilerParams(
            vmem_limit_bytes=VMEM_LIMIT, collective_id=1, has_side_effects=True
        ),
    )(dealt.reshape(-1), node_features, gain_row, w_qkv)
    incoming = incoming.reshape(slots_all, BLOCK, kv_width)
    layer_output, grad_queries, own, returning = run(
        attend_kernel,
        (my_slots, counts),
        (queries, kv_local, incoming, x_mine, d_mine),
        (
            shape((row_count, col_count), BF16),
            shape((row_count, col_count), BF16),
            shape((block_count, BLOCK, kv_width), F32),
            shape((slots_all, BLOCK, kv_width), BF16),
        ),
    )
    hbm = pl.BlockSpec(memory_space=pl.ANY)
    near_terms, relay_terms = pl.pallas_call(
        return_kernel,
        out_shape=(
            shape((half, capacity, BLOCK, kv_width), BF16),
            shape((block_count, BLOCK, kv_width), BF16),
        ),
        in_specs=[pl.BlockSpec(memory_space=pltpu.SMEM), vmem],
        out_specs=(hbm, hbm),
        scratch_shapes=[
            pltpu.VMEM((half - 1, capacity, BLOCK, kv_width), BF16),
            pltpu.VMEM((block_count, BLOCK, kv_width), BF16),
            dma((half - 1,)),
            dma((half - 1,)),
            dma((half - 1,)),
            dma((half - 1,)),
            dma,
            dma,
            dma,
        ],
        compiler_params=pltpu.CompilerParams(
            vmem_limit_bytes=VMEM_LIMIT, collective_id=2, has_side_effects=True
        ),
    )(far_from, returning.reshape(seq_count, capacity, BLOCK, kv_width))
    near_terms = near_terms.reshape(half * capacity, BLOCK, kv_width)
    share = width // seq_count
    grads, weight_parts = run(
        functools.partial(gather_kernel, node_count=row_count * seq_count),
        (near_from,),
        (own, near_terms, relay_terms, grad_queries, normed),
        (
            shape((row_count, 3 * col_count), BF16),
            shape((seq_count, 3, share, col_count), BF16),
        ),
        scratch=(
            pltpu.VMEM((block_count, BLOCK, kv_width), F32),
            pltpu.VMEM((width, 3 * col_count), F32),
        ),
    )
    others = head_count - 1
    chunks = row_count // CHUNK
    grad_input, grad_weights = run(
        exchange_kernel,
        (),
        (grads, weight_parts, node_features, x_mine, d_mine, gain_row, gain_mine, w_qkv),
        (
            shape((row_count, col_count), BF16),
            shape((3, share, col_count), F32),
        ),
        scratch=(
            pltpu.VMEM((width, 3 * col_count), BF16),
            pltpu.VMEM((head_count, row_count, col_count), BF16),
            pltpu.VMEM((others, row_count, col_count), BF16),
            pltpu.VMEM((block_count, 8, BLOCK), F32),
            pltpu.VMEM((others, block_count, 8, BLOCK), F32),
            pltpu.VMEM((seq_count - 1, 3, share, col_count), BF16),
            dma((others, chunks)),
            dma((others, chunks)),
            dma((others,)),
            dma((others,)),
            dma((seq_count - 1,)),
            dma((seq_count - 1,)),
        ),
        collective_id=0,
        has_side_effects=True,
    )
    return (layer_output, grad_input, grad_weights)


def solution(mesh):
    in_specs = (P("seq", None), P(), P(None, None, "head"), P("seq", None), P(), P("seq"))
    out_specs = (P("seq", "head"), P("seq", "head"), P(None, "seq", "head"))
    return jax.shard_map(shards, mesh=mesh, in_specs=in_specs, out_specs=out_specs, check_vma=False)
```

```python
import functools
import math

import jax
import jax.numpy as jnp
from jax import lax
from jax.experimental import pallas as pl
from jax.experimental.pallas import tpu as pltpu
from jax.sharding import PartitionSpec as P

HEAD_DIM = 64
BLOCK = 128
EXPD = 3
CHUNK = 256


EPS = 1e-06
F32 = jnp.float32
BF16 = jnp.bfloat16
VMEM_LIMIT = 50 * 1024 * 1024

CONTRACT_COLS = (((1,), (1,)), ((), ()))
CONTRACT_ROWS = (((0,), (0,)), ((), ()))


def rows_of(index, size):
    return pl.ds(pl.multiple_of(index * size, size), size)


def join_weights(w_ref, joined, cols):
    for member in range(3):
        joined[:, member * cols : (member + 1) * cols] = w_ref[member]


def project_kernel(
    sent_from,
    x_ref,
    gain_ref,
    w_ref,
    normed_ref,
    q_ref,
    kv_ref,
    in_ref,
    joined,
    relayed,
    near,
    far,
    relay_send,
    relay_recv,
    near_send,
    near_recv,
    far_send,
    far_recv,
    local_sem,
):
    cols = w_ref.shape[2]
    per_chunk = CHUNK // BLOCK
    seq_count, capacity = in_ref.shape[:2]
    half = seq_count // 2
    seq = lax.axis_index("seq")
    across = lax.rem(seq + half, seq_count)
    base = (seq // half) * half
    mesh_type = pl.DeviceIdType.MESH

    def mate(k):
        return base + lax.rem(seq - base + k, half)

    barrier = pltpu.get_barrier_semaphore()
    pl.semaphore_signal(barrier, inc=1, device_id={"seq": across}, device_id_type=mesh_type)
    for k in range(1, half):
        pl.semaphore_signal(barrier, inc=1, device_id={"seq": mate(k)}, device_id_type=mesh_type)

    join_weights(w_ref, joined, cols)
    pl.semaphore_wait(barrier, half)

    def relay(step):
        blocks = pl.ds(step * per_chunk, per_chunk)
        return pltpu.make_async_remote_copy(
            src_ref=kv_ref.at[blocks],
            dst_ref=relayed.at[blocks],
            send_sem=relay_send.at[step],
            recv_sem=relay_recv.at[step],
            device_id={"seq": across},
            device_id_type=mesh_type,
        )

    def project(step, carry):
        rows = rows_of(step, CHUNK)
        x = x_ref[rows, :].astype(F32)
        inv_rms = lax.rsqrt(jnp.mean(x * x, axis=1, keepdims=True) + EPS)
        normed = (x * inv_rms * gain_ref[...]).astype(BF16)
        normed_ref[rows, :] = normed
        made = jnp.dot(normed, joined[...], preferred_element_type=F32).astype(BF16)
        q_ref[rows, :] = made[:, :cols]
        kv_ref[pl.ds(step * per_chunk, per_chunk)] = made[:, cols:].reshape(
            per_chunk, BLOCK, 2 * cols
        )
        relay(step).start()
        return carry

    lax.fori_loop(0, x_ref.shape[0] // CHUNK, project, 0)
    def deal(source, which, owner, stage, send, recv):
        sends = []
        for k in list(range(1, half)) + [0]:
            for rank in range(capacity):
                place = sent_from[(which * seq_count + mate(k)) * capacity + rank]
                stage[k, rank] = source[place]
            if k:
                copy = pltpu.make_async_remote_copy(
                    src_ref=stage.at[k],
                    dst_ref=in_ref.at[owner],
                    send_sem=send.at[k - 1],
                    recv_sem=recv.at[k - 1],
                    device_id={"seq": mate(k)},
                    device_id_type=mesh_type,
                )
            else:
                copy = pltpu.make_async_copy(stage.at[0], in_ref.at[owner], local_sem.at[which])
            copy.start()
            sends.append(copy)
        return sends

    sends = deal(kv_ref, 0, seq, near, near_send, near_recv)

    def relay_wait(step, carry):
        relay(step).wait()
        return carry

    lax.fori_loop(0, x_ref.shape[0] // CHUNK, relay_wait, 0)
    sends += deal(relayed, 1, across, far, far_send, far_recv)
    for copy in sends:
        copy.wait()


def attend_kernel(
    slots, counts, q_ref, kv_ref, slot_ref, x_ref, d_ref, layer_ref, gq_ref, own_ref, back_ref
):
    cols = q_ref.shape[1]
    heads_here = cols // HEAD_DIM
    scale = 1.0 / math.sqrt(HEAD_DIM)
    keys_all = (1 + EXPD) * BLOCK
    lane_head = lax.broadcasted_iota(jnp.int32, (BLOCK, cols), 1) // HEAD_DIM
    key_place = lax.broadcasted_iota(jnp.int32, (1, keys_all), 1)

    def spread(value):
        return jnp.concatenate(
            [jnp.where(lane_head == h, value, jnp.zeros_like(value)) for h in range(heads_here)],
            axis=0,
        )

    def merge(value):
        made = value[:BLOCK]
        for h in range(1, heads_here):
            made = jnp.where(lane_head == h, value[h * BLOCK : (h + 1) * BLOCK], made)
        return made

    def block_step(block, carry):
        rows = rows_of(block, BLOCK)
        places = [slots[block * EXPD + j] for j in range(EXPD)]
        own = kv_ref[block]
        listed = jnp.concatenate([own] + [slot_ref[place] for place in places], axis=0)
        keys = listed[:, :cols]
        values = listed[:, cols:]
        queries = spread(q_ref[rows, :])
        grads = spread(d_ref[rows, :])
        scores = lax.dot_general(queries, keys, CONTRACT_COLS, preferred_element_type=F32) * scale
        scores = jnp.where(key_place < (counts[block] + 1) * BLOCK, scores, -jnp.inf)
        powers = jnp.exp(scores - jnp.max(scores, axis=1, keepdims=True))
        attention = powers * (1.0 / jnp.sum(powers, axis=1, keepdims=True))
        low = attention.astype(BF16)
        attended = jnp.dot(low, values, preferred_element_type=F32)
        layer_ref[rows, :] = (x_ref[rows, :].astype(F32) + merge(attended)).astype(BF16)
        grad_attention = lax.dot_general(grads, values, CONTRACT_COLS, preferred_element_type=F32)
        row_dot = jnp.sum(grads.astype(F32) * attended, axis=1, keepdims=True)
        grad_scores = (attention * (grad_attention - row_dot) * scale).astype(BF16)
        gq_ref[rows, :] = merge(jnp.dot(grad_scores, keys, preferred_element_type=F32)).astype(BF16)
        grad_keys = lax.dot_general(grad_scores, queries, CONTRACT_ROWS, preferred_element_type=F32)
        grad_values = lax.dot_general(low, grads, CONTRACT_ROWS, preferred_element_type=F32)
        own_ref[block] = jnp.concatenate([grad_keys[:BLOCK], grad_values[:BLOCK]], axis=1)
        for j, place in enumerate(places):
            part = slice((j + 1) * BLOCK, (j + 2) * BLOCK)
            back_ref[place] = jnp.concatenate([grad_keys[part], grad_values[part]], axis=1).astype(
                BF16
            )
        return carry

    lax.fori_loop(0, kv_ref.shape[0], block_step, 0)


def return_kernel(
    far_from,
    back_ref,
    near_ref,
    relay_ref,
    far_in,
    summed,
    far_send,
    far_recv,
    near_send,
    near_recv,
    relay_send,
    relay_recv,
    local_sem,
):
    seq_count, capacity = back_ref.shape[:2]
    block_count = relay_ref.shape[0]
    half = seq_count // 2
    piece = BLOCK // 2
    seq = lax.axis_index("seq")
    across = lax.rem(seq + half, seq_count)
    base = (seq // half) * half
    mesh_type = pl.DeviceIdType.MESH

    def mate(k):
        return base + lax.rem(seq - base + k, half)

    barrier = pltpu.get_barrier_semaphore()
    pl.semaphore_signal(barrier, inc=1, device_id={"seq": across}, device_id_type=mesh_type)
    for k in range(1, half):
        pl.semaphore_signal(barrier, inc=1, device_id={"seq": mate(k)}, device_id_type=mesh_type)
    pl.semaphore_wait(barrier, half)

    fars = []
    nears = []
    for k in range(1, half):
        fars.append(
            pltpu.make_async_remote_copy(
                src_ref=back_ref.at[lax.rem(mate(k) + half, seq_count)],
                dst_ref=far_in.at[k - 1],
                send_sem=far_send.at[k - 1],
                recv_sem=far_recv.at[k - 1],
                device_id={"seq": mate(k)},
                device_id_type=mesh_type,
            )
        )
        nears.append(
            pltpu.make_async_remote_copy(
                src_ref=back_ref.at[mate(k)],
                dst_ref=near_ref.at[k],
                send_sem=near_send.at[k - 1],
                recv_sem=near_recv.at[k - 1],
                device_id={"seq": mate(k)},
                device_id_type=mesh_type,
            )
        )
    nears.append(pltpu.make_async_copy(back_ref.at[seq], near_ref.at[0], local_sem))
    for copy in fars:
        copy.start()
    for copy in fars:
        copy.wait()
    for copy in nears:
        copy.start()

    def relay(block):
        return pltpu.make_async_remote_copy(
            src_ref=summed.at[block],
            dst_ref=relay_ref.at[block],
            send_sem=relay_send.at[block],
            recv_sem=relay_recv.at[block],
            device_id={"seq": across},
            device_id_type=mesh_type,
        )

    def add_block(block, carry):
        for part in range(2):
            rows = slice(part * piece, (part + 1) * piece)
            made = jnp.zeros((piece, back_ref.shape[3]), F32)
            for k in range(half):
                for rank in range(capacity):
                    if k:
                        term = far_in[k - 1, rank, rows, :]
                    else:
                        term = back_ref[across, rank, rows, :]
                    listed = far_from[k * capacity + rank] == block
                    made = made + jnp.where(listed, term.astype(F32), 0.0)
            summed[block, rows, :] = made.astype(BF16)
        relay(block).start()
        return carry

    def relay_wait(block, carry):
        relay(block).wait()
        return carry

    lax.fori_loop(0, block_count, add_block, 0)
    for copy in nears:
        copy.wait()
    lax.fori_loop(0, block_count, relay_wait, 0)


def gather_kernel(
    near_from,
    own_ref,
    near_ref,
    relay_ref,
    gq_ref,
    normed_ref,
    grads_ref,
    gw_ref,
    total,
    sums,
    *,
    node_count,
):
    cols = gq_ref.shape[1]
    width = normed_ref.shape[1]
    per_chunk = CHUNK // BLOCK
    sums[...] = jnp.zeros_like(sums)
    total[...] = own_ref[...] + relay_ref[...].astype(F32)

    def gather(slot, carry):
        place = near_from[slot]

        @pl.when(place >= 0)
        def _():
            total[place] = total[place] + near_ref[slot].astype(F32)

        return carry

    lax.fori_loop(0, near_ref.shape[0], gather, 0)

    def chunk_step(step, carry):
        rows = rows_of(step, CHUNK)
        grad_kv = total[pl.ds(step * per_chunk, per_chunk)].reshape(CHUNK, 2 * cols).astype(BF16)
        grads = jnp.concatenate([gq_ref[rows, :], grad_kv], axis=1)
        grads_ref[rows, :] = grads
        sums[...] += lax.dot_general(
            normed_ref[rows, :], grads, CONTRACT_ROWS, preferred_element_type=F32
        )
        return carry

    lax.fori_loop(0, gq_ref.shape[0] // CHUNK, chunk_step, 0)
    seq_count = gw_ref.shape[0]
    share = width // seq_count
    factor = 1.0 / math.sqrt(node_count)
    for peer in range(seq_count):
        for member in range(3):
            gw_ref[peer, member] = (
                sums[peer * share : (peer + 1) * share, member * cols : (member + 1) * cols]
                * factor
            ).astype(BF16)


def exchange_kernel(
    grads_ref,
    gw_ref,
    x_ref,
    mine_ref,
    d_ref,
    gain_ref,
    gain_mine_ref,
    w_ref,
    out_ref,
    weights_ref,
    joined,
    parts,
    arrived,
    terms,
    terms_in,
    gw_in,
    part_send,
    part_recv,
    term_send,
    term_recv,
    gw_send,
    gw_recv,
):
    cols = w_ref.shape[2]
    row_count, width = x_ref.shape
    head_count = parts.shape[0]
    seq_count = gw_ref.shape[0]
    per_chunk = CHUNK // BLOCK
    chunks = row_count // CHUNK
    head = lax.axis_index("head")
    seq = lax.axis_index("seq")
    mesh_type = pl.DeviceIdType.MESH

    def head_peer(k):
        return lax.rem(head + k, head_count)

    def seq_peer(k):
        return lax.rem(seq + k, seq_count)

    barrier = pltpu.get_barrier_semaphore()
    for k in range(1, head_count):
        pl.semaphore_signal(
            barrier, inc=1, device_id={"head": head_peer(k)}, device_id_type=mesh_type
        )
    for k in range(1, seq_count):
        pl.semaphore_signal(
            barrier, inc=1, device_id={"seq": seq_peer(k)}, device_id_type=mesh_type
        )
    pl.semaphore_wait(barrier, head_count + seq_count - 2)

    def weight_copy(k):
        return pltpu.make_async_remote_copy(
            src_ref=gw_ref.at[seq_peer(k)],
            dst_ref=gw_in.at[k - 1],
            send_sem=gw_send.at[k - 1],
            recv_sem=gw_recv.at[k - 1],
            device_id={"seq": seq_peer(k)},
            device_id_type=mesh_type,
        )

    def part_copy(k, step):
        rows = rows_of(step, CHUNK)
        return pltpu.make_async_remote_copy(
            src_ref=parts.at[head_peer(k), rows],
            dst_ref=arrived.at[k - 1, rows],
            send_sem=part_send.at[k - 1, step],
            recv_sem=part_recv.at[k - 1, step],
            device_id={"head": head_peer(k)},
            device_id_type=mesh_type,
        )

    def term_copy(k):
        return pltpu.make_async_remote_copy(
            src_ref=terms,
            dst_ref=terms_in.at[k - 1],
            send_sem=term_send.at[k - 1],
            recv_sem=term_recv.at[k - 1],
            device_id={"head": head_peer(k)},
            device_id_type=mesh_type,
        )

    for k in range(1, seq_count):
        weight_copy(k).start()
    join_weights(w_ref, joined, cols)

    def chunk_step(step, carry):
        rows = rows_of(step, CHUNK)
        grad_normed = lax.dot_general(
            grads_ref[rows, :], joined[...], CONTRACT_COLS, preferred_element_type=F32
        )
        for part in range(head_count):
            parts[part, rows, :] = grad_normed[:, part * cols : (part + 1) * cols].astype(BF16)
        for k in range(1, head_count):
            part_copy(k, step).start()
        term = jnp.sum(
            x_ref[rows, :].astype(F32) * gain_ref[...] * grad_normed, axis=1, keepdims=True
        )
        for inner in range(per_chunk):
            piece = jnp.broadcast_to(term[inner * BLOCK : (inner + 1) * BLOCK], (BLOCK, BLOCK))
            terms[step * per_chunk + inner] = piece.T[:8]
        return carry

    lax.fori_loop(0, chunks, chunk_step, 0)
    for k in range(1, head_count):
        term_copy(k).start()
    for k in range(1, seq_count):
        weight_copy(k).wait()
    total = gw_ref[seq].astype(F32)
    for k in range(1, seq_count):
        total = total + gw_in[k - 1].astype(F32)
    weights_ref[...] = total
    for k in range(1, head_count):
        term_copy(k).wait()

    def final_step(step, carry):
        rows = rows_of(step, CHUNK)
        x = x_ref[rows, :].astype(F32)
        inv_rms = lax.rsqrt(jnp.mean(x * x, axis=1, keepdims=True) + EPS)
        columns = []
        for inner in range(per_chunk):
            row = terms[step * per_chunk + inner]
            for k in range(1, head_count):
                row = row + terms_in[k - 1, step * per_chunk + inner]
            columns.append(jnp.broadcast_to(row[:1], (BLOCK, BLOCK)).T[:, :1])
        term = jnp.concatenate(columns, axis=0) * (1.0 / width)
        for k in range(1, head_count):
            part_copy(k, step).wait()
        grad = parts[head, rows, :].astype(F32)
        for k in range(1, head_count):
            grad = grad + arrived[k - 1, rows, :].astype(F32)
        cubed = inv_rms * inv_rms * inv_rms
        out_ref[rows, :] = (
            d_ref[rows, :].astype(F32)
            + inv_rms * gain_mine_ref[...] * grad
            - mine_ref[rows, :].astype(F32) * (cubed * term)
        ).astype(BF16)
        return carry

    lax.fori_loop(0, chunks, final_step, 0)


def whole(shape):
    return pl.BlockSpec(shape, lambda i, *refs: (0,) * len(shape))


def run(kernel, scalars, args, outs, scratch=(), **params):
    return pl.pallas_call(
        kernel,
        out_shape=outs,
        grid_spec=pltpu.PrefetchScalarGridSpec(
            num_scalar_prefetch=len(scalars),
            grid=(1,),
            in_specs=[whole(value.shape) for value in args],
            out_specs=jax.tree.map(lambda out: whole(out.shape), outs),
            scratch_shapes=list(scratch),
        ),
        compiler_params=pltpu.CompilerParams(vmem_limit_bytes=VMEM_LIMIT, **params),
    )(*scalars, *args)


def shards(node_features, gain, w_qkv, d_out, pattern, counts):
    seq_count = lax.axis_size("seq")
    my_index = lax.axis_index("seq")
    row_count, width = node_features.shape
    block_count = row_count // BLOCK
    col_count = w_qkv.shape[2]
    head_count = width // col_count
    slot_count = block_count * EXPD
    capacity = max(2, 3 * slot_count // (2 * seq_count))
    slots_all = seq_count * capacity
    kv_width = 2 * col_count
    col_start = lax.axis_index("head") * col_count
    gain_row = gain.reshape(1, width)
    x_mine, d_mine, gain_mine = (
        lax.dynamic_slice_in_dim(value, col_start, col_count, 1)
        for value in (node_features, d_out, gain_row)
    )
    shape = jax.ShapeDtypeStruct

    owners = (pattern // block_count).reshape(seq_count, slot_count)
    in_owner = (pattern % block_count).reshape(seq_count, slot_count)
    before = jnp.arange(slot_count)[:, None] > jnp.arange(slot_count)[None, :]
    same = owners[:, :, None] == owners[:, None, :]
    ranks = jnp.sum((same & before[None]).astype(jnp.int32), axis=2)
    places = jnp.arange(capacity, dtype=jnp.int32)
    peers = jnp.arange(seq_count, dtype=jnp.int32)
    half = seq_count // 2
    holders = jnp.stack([my_index, (my_index + half) % seq_count]).astype(jnp.int32)
    picked = (owners[None, :, None, :] == holders[:, None, None, None]) & (
        ranks[None, :, None, :] == places[None, None, :, None]
    )
    dealt = jnp.sum(jnp.where(picked, in_owner[None, :, None, :], 0), axis=3)
    taken = jnp.where(jnp.any(picked, axis=3), dealt, -1)
    base = (my_index // half) * half
    senders = base + (my_index - base - jnp.arange(half, dtype=jnp.int32)) % half
    near_from, far_from = (
        jnp.sum(
            jnp.where(
                senders[:, None, None] == peers[None, :, None], taken[which][None], 0
            ),
            axis=1,
        ).reshape(-1)
        for which in range(2)
    )
    my_slots = lax.dynamic_index_in_dim(owners * capacity + ranks, my_index, 0, keepdims=False)

    dma = pltpu.SemaphoreType.DMA
    vmem = pl.BlockSpec(memory_space=pltpu.VMEM)
    normed, queries, kv_local, incoming = pl.pallas_call(
        project_kernel,
        out_shape=(
            shape((row_count, width), BF16),
            shape((row_count, col_count), BF16),
            shape((block_count, BLOCK, kv_width), BF16),
            shape((seq_count, capacity, BLOCK, kv_width), BF16),
        ),
        in_specs=[pl.BlockSpec(memory_space=pltpu.SMEM), vmem, vmem, vmem],
        out_specs=(vmem, vmem, vmem, pl.BlockSpec(memory_space=pl.ANY)),
        scratch_shapes=[
            pltpu.VMEM((width, 3 * col_count), BF16),
            pltpu.VMEM((block_count, BLOCK, kv_width), BF16),
            pltpu.VMEM((half, capacity, BLOCK, kv_width), BF16),
            pltpu.VMEM((half, capacity, BLOCK, kv_width), BF16),
            dma((row_count // CHUNK,)),
            dma((row_count // CHUNK,)),
            dma((half - 1,)),
            dma((half - 1,)),
            dma((half - 1,)),
            dma((half - 1,)),
            dma((2,)),
        ],
        compiler_params=pltpu.CompilerParams(
            vmem_limit_bytes=VMEM_LIMIT, collective_id=1, has_side_effects=True
        ),
    )(dealt.reshape(-1), node_features, gain_row, w_qkv)
    incoming = incoming.reshape(slots_all, BLOCK, kv_width)
    layer_output, grad_queries, own, returning = run(
        attend_kernel,
        (my_slots, counts),
        (queries, kv_local, incoming, x_mine, d_mine),
        (
            shape((row_count, col_count), BF16),
            shape((row_count, col_count), BF16),
            shape((block_count, BLOCK, kv_width), F32),
            shape((slots_all, BLOCK, kv_width), BF16),
        ),
    )
    hbm = pl.BlockSpec(memory_space=pl.ANY)
    near_terms, relay_terms = pl.pallas_call(
        return_kernel,
        out_shape=(
            shape((half, capacity, BLOCK, kv_width), BF16),
            shape((block_count, BLOCK, kv_width), BF16),
        ),
        in_specs=[pl.BlockSpec(memory_space=pltpu.SMEM), vmem],
        out_specs=(hbm, hbm),
        scratch_shapes=[
            pltpu.VMEM((half - 1, capacity, BLOCK, kv_width), BF16),
            pltpu.VMEM((block_count, BLOCK, kv_width), BF16),
            dma((half - 1,)),
            dma((half - 1,)),
            dma((half - 1,)),
            dma((half - 1,)),
            dma((block_count,)),
            dma((block_count,)),
            dma,
        ],
        compiler_params=pltpu.CompilerParams(
            vmem_limit_bytes=VMEM_LIMIT, collective_id=2, has_side_effects=True
        ),
    )(far_from, returning.reshape(seq_count, capacity, BLOCK, kv_width))
    near_terms = near_terms.reshape(half * capacity, BLOCK, kv_width)
    share = width // seq_count
    grads, weight_parts = run(
        functools.partial(gather_kernel, node_count=row_count * seq_count),
        (near_from,),
        (own, near_terms, relay_terms, grad_queries, normed),
        (
            shape((row_count, 3 * col_count), BF16),
            shape((seq_count, 3, share, col_count), BF16),
        ),
        scratch=(
            pltpu.VMEM((block_count, BLOCK, kv_width), F32),
            pltpu.VMEM((width, 3 * col_count), F32),
        ),
    )
    others = head_count - 1
    chunks = row_count // CHUNK
    grad_input, grad_weights = run(
        exchange_kernel,
        (),
        (grads, weight_parts, node_features, x_mine, d_mine, gain_row, gain_mine, w_qkv),
        (
            shape((row_count, col_count), BF16),
            shape((3, share, col_count), F32),
        ),
        scratch=(
            pltpu.VMEM((width, 3 * col_count), BF16),
            pltpu.VMEM((head_count, row_count, col_count), BF16),
            pltpu.VMEM((others, row_count, col_count), BF16),
            pltpu.VMEM((block_count, 8, BLOCK), F32),
            pltpu.VMEM((others, block_count, 8, BLOCK), F32),
            pltpu.VMEM((seq_count - 1, 3, share, col_count), BF16),
            dma((others, chunks)),
            dma((others, chunks)),
            dma((others,)),
            dma((others,)),
            dma((seq_count - 1,)),
            dma((seq_count - 1,)),
        ),
        collective_id=0,
        has_side_effects=True,
    )
    return (layer_output, grad_input, grad_weights)


def solution(mesh):
    in_specs = (P("seq", None), P(), P(None, None, "head"), P("seq", None), P(), P("seq"))
    out_specs = (P("seq", "head"), P("seq", "head"), P(None, "seq", "head"))
    return jax.shard_map(shards, mesh=mesh, in_specs=in_specs, out_specs=out_specs, check_vma=False)
```

```python
import functools
import math

import jax
import jax.numpy as jnp
from jax import lax
from jax.experimental import pallas as pl
from jax.experimental.pallas import tpu as pltpu
from jax.sharding import PartitionSpec as P

HEAD_DIM = 64
BLOCK = 128
EXPD = 3
CHUNK = 256


EPS = 1e-06
F32 = jnp.float32
BF16 = jnp.bfloat16
VMEM_LIMIT = 50 * 1024 * 1024

CONTRACT_COLS = (((1,), (1,)), ((), ()))
CONTRACT_ROWS = (((0,), (0,)), ((), ()))


def rows_of(index, size):
    return pl.ds(pl.multiple_of(index * size, size), size)


def join_weights(w_ref, joined, cols):
    for member in range(3):
        joined[:, member * cols : (member + 1) * cols] = w_ref[member]


def project_kernel(
    sent_from,
    x_ref,
    gain_ref,
    w_ref,
    normed_ref,
    q_ref,
    kv_ref,
    in_ref,
    joined,
    relayed,
    near,
    far,
    relay_send,
    relay_recv,
    near_send,
    near_recv,
    far_send,
    far_recv,
    local_sem,
):
    cols = w_ref.shape[2]
    per_chunk = CHUNK // BLOCK
    seq_count, capacity = in_ref.shape[:2]
    half = seq_count // 2
    seq = lax.axis_index("seq")
    across = lax.rem(seq + half, seq_count)
    base = (seq // half) * half
    mesh_type = pl.DeviceIdType.MESH

    def mate(k):
        return base + lax.rem(seq - base + k, half)

    barrier = pltpu.get_barrier_semaphore()
    pl.semaphore_signal(barrier, inc=1, device_id={"seq": across}, device_id_type=mesh_type)
    for k in range(1, half):
        pl.semaphore_signal(barrier, inc=1, device_id={"seq": mate(k)}, device_id_type=mesh_type)

    join_weights(w_ref, joined, cols)
    pl.semaphore_wait(barrier, half)

    def relay(step):
        blocks = pl.ds(step * per_chunk, per_chunk)
        return pltpu.make_async_remote_copy(
            src_ref=kv_ref.at[blocks],
            dst_ref=relayed.at[blocks],
            send_sem=relay_send.at[step],
            recv_sem=relay_recv.at[step],
            device_id={"seq": across},
            device_id_type=mesh_type,
        )

    def project(step, carry):
        rows = rows_of(step, CHUNK)
        x = x_ref[rows, :].astype(F32)
        inv_rms = lax.rsqrt(jnp.mean(x * x, axis=1, keepdims=True) + EPS)
        normed = (x * inv_rms * gain_ref[...]).astype(BF16)
        normed_ref[rows, :] = normed
        made = jnp.dot(normed, joined[...], preferred_element_type=F32).astype(BF16)
        q_ref[rows, :] = made[:, :cols]
        kv_ref[pl.ds(step * per_chunk, per_chunk)] = made[:, cols:].reshape(
            per_chunk, BLOCK, 2 * cols
        )
        relay(step).start()
        return carry

    lax.fori_loop(0, x_ref.shape[0] // CHUNK, project, 0)
    def deal(source, which, owner, stage, send, recv):
        sends = []
        for k in list(range(1, half)) + [0]:
            for rank in range(capacity):
                place = sent_from[(which * seq_count + mate(k)) * capacity + rank]
                stage[k, rank] = source[place]
            if k:
                copy = pltpu.make_async_remote_copy(
                    src_ref=stage.at[k],
                    dst_ref=in_ref.at[owner],
                    send_sem=send.at[k - 1],
                    recv_sem=recv.at[k - 1],
                    device_id={"seq": mate(k)},
                    device_id_type=mesh_type,
                )
            else:
                copy = pltpu.make_async_copy(stage.at[0], in_ref.at[owner], local_sem.at[which])
            copy.start()
            sends.append(copy)
        return sends

    sends = deal(kv_ref, 0, seq, near, near_send, near_recv)

    def relay_wait(step, carry):
        relay(step).wait()
        return carry

    lax.fori_loop(0, x_ref.shape[0] // CHUNK, relay_wait, 0)
    sends += deal(relayed, 1, across, far, far_send, far_recv)
    for copy in sends:
        copy.wait()


def attend_kernel(
    slots, counts, q_ref, kv_ref, slot_ref, x_ref, d_ref, layer_ref, gq_ref, own_ref, back_ref
):
    cols = q_ref.shape[1]
    heads_here = cols // HEAD_DIM
    scale = 1.0 / math.sqrt(HEAD_DIM)
    keys_all = (1 + EXPD) * BLOCK
    lane_head = lax.broadcasted_iota(jnp.int32, (BLOCK, cols), 1) // HEAD_DIM
    key_place = lax.broadcasted_iota(jnp.int32, (1, keys_all), 1)

    def spread(value):
        return jnp.concatenate(
            [jnp.where(lane_head == h, value, jnp.zeros_like(value)) for h in range(heads_here)],
            axis=0,
        )

    def merge(value):
        made = value[:BLOCK]
        for h in range(1, heads_here):
            made = jnp.where(lane_head == h, value[h * BLOCK : (h + 1) * BLOCK], made)
        return made

    def block_step(block, carry):
        rows = rows_of(block, BLOCK)
        places = [slots[block * EXPD + j] for j in range(EXPD)]
        own = kv_ref[block]
        listed = jnp.concatenate([own] + [slot_ref[place] for place in places], axis=0)
        keys = listed[:, :cols]
        values = listed[:, cols:]
        queries = spread(q_ref[rows, :])
        grads = spread(d_ref[rows, :])
        scores = lax.dot_general(queries, keys, CONTRACT_COLS, preferred_element_type=F32) * scale
        scores = jnp.where(key_place < (counts[block] + 1) * BLOCK, scores, -jnp.inf)
        powers = jnp.exp(scores - jnp.max(scores, axis=1, keepdims=True))
        attention = powers * (1.0 / jnp.sum(powers, axis=1, keepdims=True))
        low = attention.astype(BF16)
        attended = jnp.dot(low, values, preferred_element_type=F32)
        layer_ref[rows, :] = (x_ref[rows, :].astype(F32) + merge(attended)).astype(BF16)
        grad_attention = lax.dot_general(grads, values, CONTRACT_COLS, preferred_element_type=F32)
        row_dot = jnp.sum(grads.astype(F32) * attended, axis=1, keepdims=True)
        grad_scores = (attention * (grad_attention - row_dot) * scale).astype(BF16)
        gq_ref[rows, :] = merge(jnp.dot(grad_scores, keys, preferred_element_type=F32)).astype(BF16)
        grad_keys = lax.dot_general(grad_scores, queries, CONTRACT_ROWS, preferred_element_type=F32)
        grad_values = lax.dot_general(low, grads, CONTRACT_ROWS, preferred_element_type=F32)
        own_ref[block] = jnp.concatenate([grad_keys[:BLOCK], grad_values[:BLOCK]], axis=1)
        for j, place in enumerate(places):
            part = slice((j + 1) * BLOCK, (j + 2) * BLOCK)
            back_ref[place] = jnp.concatenate([grad_keys[part], grad_values[part]], axis=1).astype(
                BF16
            )
        return carry

    lax.fori_loop(0, kv_ref.shape[0], block_step, 0, unroll=2)


def return_kernel(
    far_from,
    back_ref,
    near_ref,
    relay_ref,
    far_in,
    summed,
    far_send,
    far_recv,
    near_send,
    near_recv,
    relay_send,
    relay_recv,
    local_sem,
):
    seq_count, capacity = back_ref.shape[:2]
    block_count = relay_ref.shape[0]
    half = seq_count // 2
    piece = BLOCK // 2
    seq = lax.axis_index("seq")
    across = lax.rem(seq + half, seq_count)
    base = (seq // half) * half
    mesh_type = pl.DeviceIdType.MESH

    def mate(k):
        return base + lax.rem(seq - base + k, half)

    barrier = pltpu.get_barrier_semaphore()
    pl.semaphore_signal(barrier, inc=1, device_id={"seq": across}, device_id_type=mesh_type)
    for k in range(1, half):
        pl.semaphore_signal(barrier, inc=1, device_id={"seq": mate(k)}, device_id_type=mesh_type)
    pl.semaphore_wait(barrier, half)

    fars = []
    nears = []
    for k in range(1, half):
        fars.append(
            pltpu.make_async_remote_copy(
                src_ref=back_ref.at[lax.rem(mate(k) + half, seq_count)],
                dst_ref=far_in.at[k - 1],
                send_sem=far_send.at[k - 1],
                recv_sem=far_recv.at[k - 1],
                device_id={"seq": mate(k)},
                device_id_type=mesh_type,
            )
        )
        nears.append(
            pltpu.make_async_remote_copy(
                src_ref=back_ref.at[mate(k)],
                dst_ref=near_ref.at[k],
                send_sem=near_send.at[k - 1],
                recv_sem=near_recv.at[k - 1],
                device_id={"seq": mate(k)},
                device_id_type=mesh_type,
            )
        )
    nears.append(pltpu.make_async_copy(back_ref.at[seq], near_ref.at[0], local_sem))
    for copy in fars:
        copy.start()
    for copy in fars:
        copy.wait()
    for copy in nears:
        copy.start()

    def relay(block):
        return pltpu.make_async_remote_copy(
            src_ref=summed.at[block],
            dst_ref=relay_ref.at[block],
            send_sem=relay_send.at[block],
            recv_sem=relay_recv.at[block],
            device_id={"seq": across},
            device_id_type=mesh_type,
        )

    def add_block(block, carry):
        for part in range(2):
            rows = slice(part * piece, (part + 1) * piece)
            made = jnp.zeros((piece, back_ref.shape[3]), F32)
            for k in range(half):
                for rank in range(capacity):
                    if k:
                        term = far_in[k - 1, rank, rows, :]
                    else:
                        term = back_ref[across, rank, rows, :]
                    listed = far_from[k * capacity + rank] == block
                    made = made + jnp.where(listed, term.astype(F32), 0.0)
            summed[block, rows, :] = made.astype(BF16)
        relay(block).start()
        return carry

    def relay_wait(block, carry):
        relay(block).wait()
        return carry

    lax.fori_loop(0, block_count, add_block, 0)
    for copy in nears:
        copy.wait()
    lax.fori_loop(0, block_count, relay_wait, 0)


def gather_kernel(
    near_from,
    own_ref,
    near_ref,
    relay_ref,
    gq_ref,
    normed_ref,
    grads_ref,
    gw_ref,
    total,
    sums,
    *,
    node_count,
):
    cols = gq_ref.shape[1]
    width = normed_ref.shape[1]
    per_chunk = CHUNK // BLOCK
    sums[...] = jnp.zeros_like(sums)
    total[...] = own_ref[...] + relay_ref[...].astype(F32)

    def gather(slot, carry):
        place = near_from[slot]

        @pl.when(place >= 0)
        def _():
            total[place] = total[place] + near_ref[slot].astype(F32)

        return carry

    lax.fori_loop(0, near_ref.shape[0], gather, 0)

    def chunk_step(step, carry):
        rows = rows_of(step, CHUNK)
        grad_kv = total[pl.ds(step * per_chunk, per_chunk)].reshape(CHUNK, 2 * cols).astype(BF16)
        grads = jnp.concatenate([gq_ref[rows, :], grad_kv], axis=1)
        grads_ref[rows, :] = grads
        sums[...] += lax.dot_general(
            normed_ref[rows, :], grads, CONTRACT_ROWS, preferred_element_type=F32
        )
        return carry

    lax.fori_loop(0, gq_ref.shape[0] // CHUNK, chunk_step, 0)
    seq_count = gw_ref.shape[0]
    share = width // seq_count
    factor = 1.0 / math.sqrt(node_count)
    for peer in range(seq_count):
        for member in range(3):
            gw_ref[peer, member] = (
                sums[peer * share : (peer + 1) * share, member * cols : (member + 1) * cols]
                * factor
            ).astype(BF16)


def exchange_kernel(
    grads_ref,
    gw_ref,
    x_ref,
    mine_ref,
    d_ref,
    gain_ref,
    gain_mine_ref,
    w_ref,
    out_ref,
    weights_ref,
    joined,
    parts,
    arrived,
    terms,
    terms_in,
    gw_in,
    part_send,
    part_recv,
    term_send,
    term_recv,
    gw_send,
    gw_recv,
):
    cols = w_ref.shape[2]
    row_count, width = x_ref.shape
    head_count = parts.shape[0]
    seq_count = gw_ref.shape[0]
    per_chunk = CHUNK // BLOCK
    chunks = row_count // CHUNK
    head = lax.axis_index("head")
    seq = lax.axis_index("seq")
    mesh_type = pl.DeviceIdType.MESH

    def head_peer(k):
        return lax.rem(head + k, head_count)

    def seq_peer(k):
        return lax.rem(seq + k, seq_count)

    barrier = pltpu.get_barrier_semaphore()
    for k in range(1, head_count):
        pl.semaphore_signal(
            barrier, inc=1, device_id={"head": head_peer(k)}, device_id_type=mesh_type
        )
    for k in range(1, seq_count):
        pl.semaphore_signal(
            barrier, inc=1, device_id={"seq": seq_peer(k)}, device_id_type=mesh_type
        )
    pl.semaphore_wait(barrier, head_count + seq_count - 2)

    def weight_copy(k):
        return pltpu.make_async_remote_copy(
            src_ref=gw_ref.at[seq_peer(k)],
            dst_ref=gw_in.at[k - 1],
            send_sem=gw_send.at[k - 1],
            recv_sem=gw_recv.at[k - 1],
            device_id={"seq": seq_peer(k)},
            device_id_type=mesh_type,
        )

    def part_copy(k, step):
        rows = rows_of(step, CHUNK)
        return pltpu.make_async_remote_copy(
            src_ref=parts.at[head_peer(k), rows],
            dst_ref=arrived.at[k - 1, rows],
            send_sem=part_send.at[k - 1, step],
            recv_sem=part_recv.at[k - 1, step],
            device_id={"head": head_peer(k)},
            device_id_type=mesh_type,
        )

    def term_copy(k):
        return pltpu.make_async_remote_copy(
            src_ref=terms,
            dst_ref=terms_in.at[k - 1],
            send_sem=term_send.at[k - 1],
            recv_sem=term_recv.at[k - 1],
            device_id={"head": head_peer(k)},
            device_id_type=mesh_type,
        )

    for k in range(1, seq_count):
        weight_copy(k).start()
    join_weights(w_ref, joined, cols)

    def chunk_step(step, carry):
        rows = rows_of(step, CHUNK)
        grad_normed = lax.dot_general(
            grads_ref[rows, :], joined[...], CONTRACT_COLS, preferred_element_type=F32
        )
        for part in range(head_count):
            parts[part, rows, :] = grad_normed[:, part * cols : (part + 1) * cols].astype(BF16)
        for k in range(1, head_count):
            part_copy(k, step).start()
        term = jnp.sum(
            x_ref[rows, :].astype(F32) * gain_ref[...] * grad_normed, axis=1, keepdims=True
        )
        for inner in range(per_chunk):
            piece = jnp.broadcast_to(term[inner * BLOCK : (inner + 1) * BLOCK], (BLOCK, BLOCK))
            terms[step * per_chunk + inner] = piece.T[:8]
        return carry

    lax.fori_loop(0, chunks, chunk_step, 0)
    for k in range(1, head_count):
        term_copy(k).start()
    for k in range(1, seq_count):
        weight_copy(k).wait()
    total = gw_ref[seq].astype(F32)
    for k in range(1, seq_count):
        total = total + gw_in[k - 1].astype(F32)
    weights_ref[...] = total
    for k in range(1, head_count):
        term_copy(k).wait()

    def final_step(step, carry):
        rows = rows_of(step, CHUNK)
        x = x_ref[rows, :].astype(F32)
        inv_rms = lax.rsqrt(jnp.mean(x * x, axis=1, keepdims=True) + EPS)
        columns = []
        for inner in range(per_chunk):
            row = terms[step * per_chunk + inner]
            for k in range(1, head_count):
                row = row + terms_in[k - 1, step * per_chunk + inner]
            columns.append(jnp.broadcast_to(row[:1], (BLOCK, BLOCK)).T[:, :1])
        term = jnp.concatenate(columns, axis=0) * (1.0 / width)
        for k in range(1, head_count):
            part_copy(k, step).wait()
        grad = parts[head, rows, :].astype(F32)
        for k in range(1, head_count):
            grad = grad + arrived[k - 1, rows, :].astype(F32)
        cubed = inv_rms * inv_rms * inv_rms
        out_ref[rows, :] = (
            d_ref[rows, :].astype(F32)
            + inv_rms * gain_mine_ref[...] * grad
            - mine_ref[rows, :].astype(F32) * (cubed * term)
        ).astype(BF16)
        return carry

    lax.fori_loop(0, chunks, final_step, 0)


def whole(shape):
    return pl.BlockSpec(shape, lambda i, *refs: (0,) * len(shape))


def run(kernel, scalars, args, outs, scratch=(), **params):
    return pl.pallas_call(
        kernel,
        out_shape=outs,
        grid_spec=pltpu.PrefetchScalarGridSpec(
            num_scalar_prefetch=len(scalars),
            grid=(1,),
            in_specs=[whole(value.shape) for value in args],
            out_specs=jax.tree.map(lambda out: whole(out.shape), outs),
            scratch_shapes=list(scratch),
        ),
        compiler_params=pltpu.CompilerParams(vmem_limit_bytes=VMEM_LIMIT, **params),
    )(*scalars, *args)


def shards(node_features, gain, w_qkv, d_out, pattern, counts):
    seq_count = lax.axis_size("seq")
    my_index = lax.axis_index("seq")
    row_count, width = node_features.shape
    block_count = row_count // BLOCK
    col_count = w_qkv.shape[2]
    head_count = width // col_count
    slot_count = block_count * EXPD
    capacity = max(2, 3 * slot_count // (2 * seq_count))
    slots_all = seq_count * capacity
    kv_width = 2 * col_count
    col_start = lax.axis_index("head") * col_count
    gain_row = gain.reshape(1, width)
    x_mine, d_mine, gain_mine = (
        lax.dynamic_slice_in_dim(value, col_start, col_count, 1)
        for value in (node_features, d_out, gain_row)
    )
    shape = jax.ShapeDtypeStruct

    owners = (pattern // block_count).reshape(seq_count, slot_count)
    in_owner = (pattern % block_count).reshape(seq_count, slot_count)
    before = jnp.arange(slot_count)[:, None] > jnp.arange(slot_count)[None, :]
    same = owners[:, :, None] == owners[:, None, :]
    ranks = jnp.sum((same & before[None]).astype(jnp.int32), axis=2)
    places = jnp.arange(capacity, dtype=jnp.int32)
    peers = jnp.arange(seq_count, dtype=jnp.int32)
    half = seq_count // 2
    holders = jnp.stack([my_index, (my_index + half) % seq_count]).astype(jnp.int32)
    picked = (owners[None, :, None, :] == holders[:, None, None, None]) & (
        ranks[None, :, None, :] == places[None, None, :, None]
    )
    dealt = jnp.sum(jnp.where(picked, in_owner[None, :, None, :], 0), axis=3)
    taken = jnp.where(jnp.any(picked, axis=3), dealt, -1)
    base = (my_index // half) * half
    senders = base + (my_index - base - jnp.arange(half, dtype=jnp.int32)) % half
    near_from, far_from = (
        jnp.sum(
            jnp.where(
                senders[:, None, None] == peers[None, :, None], taken[which][None], 0
            ),
            axis=1,
        ).reshape(-1)
        for which in range(2)
    )
    my_slots = lax.dynamic_index_in_dim(owners * capacity + ranks, my_index, 0, keepdims=False)

    dma = pltpu.SemaphoreType.DMA
    vmem = pl.BlockSpec(memory_space=pltpu.VMEM)
    normed, queries, kv_local, incoming = pl.pallas_call(
        project_kernel,
        out_shape=(
            shape((row_count, width), BF16),
            shape((row_count, col_count), BF16),
            shape((block_count, BLOCK, kv_width), BF16),
            shape((seq_count, capacity, BLOCK, kv_width), BF16),
        ),
        in_specs=[pl.BlockSpec(memory_space=pltpu.SMEM), vmem, vmem, vmem],
        out_specs=(vmem, vmem, vmem, pl.BlockSpec(memory_space=pl.ANY)),
        scratch_shapes=[
            pltpu.VMEM((width, 3 * col_count), BF16),
            pltpu.VMEM((block_count, BLOCK, kv_width), BF16),
            pltpu.VMEM((half, capacity, BLOCK, kv_width), BF16),
            pltpu.VMEM((half, capacity, BLOCK, kv_width), BF16),
            dma((row_count // CHUNK,)),
            dma((row_count // CHUNK,)),
            dma((half - 1,)),
            dma((half - 1,)),
            dma((half - 1,)),
            dma((half - 1,)),
            dma((2,)),
        ],
        compiler_params=pltpu.CompilerParams(
            vmem_limit_bytes=VMEM_LIMIT, collective_id=1, has_side_effects=True
        ),
    )(dealt.reshape(-1), node_features, gain_row, w_qkv)
    incoming = incoming.reshape(slots_all, BLOCK, kv_width)
    layer_output, grad_queries, own, returning = run(
        attend_kernel,
        (my_slots, counts),
        (queries, kv_local, incoming, x_mine, d_mine),
        (
            shape((row_count, col_count), BF16),
            shape((row_count, col_count), BF16),
            shape((block_count, BLOCK, kv_width), F32),
            shape((slots_all, BLOCK, kv_width), BF16),
        ),
    )
    hbm = pl.BlockSpec(memory_space=pl.ANY)
    near_terms, relay_terms = pl.pallas_call(
        return_kernel,
        out_shape=(
            shape((half, capacity, BLOCK, kv_width), BF16),
            shape((block_count, BLOCK, kv_width), BF16),
        ),
        in_specs=[pl.BlockSpec(memory_space=pltpu.SMEM), vmem],
        out_specs=(hbm, hbm),
        scratch_shapes=[
            pltpu.VMEM((half - 1, capacity, BLOCK, kv_width), BF16),
            pltpu.VMEM((block_count, BLOCK, kv_width), BF16),
            dma((half - 1,)),
            dma((half - 1,)),
            dma((half - 1,)),
            dma((half - 1,)),
            dma((block_count,)),
            dma((block_count,)),
            dma,
        ],
        compiler_params=pltpu.CompilerParams(
            vmem_limit_bytes=VMEM_LIMIT, collective_id=2, has_side_effects=True
        ),
    )(far_from, returning.reshape(seq_count, capacity, BLOCK, kv_width))
    near_terms = near_terms.reshape(half * capacity, BLOCK, kv_width)
    share = width // seq_count
    grads, weight_parts = run(
        functools.partial(gather_kernel, node_count=row_count * seq_count),
        (near_from,),
        (own, near_terms, relay_terms, grad_queries, normed),
        (
            shape((row_count, 3 * col_count), BF16),
            shape((seq_count, 3, share, col_count), BF16),
        ),
        scratch=(
            pltpu.VMEM((block_count, BLOCK, kv_width), F32),
            pltpu.VMEM((width, 3 * col_count), F32),
        ),
    )
    others = head_count - 1
    chunks = row_count // CHUNK
    grad_input, grad_weights = run(
        exchange_kernel,
        (),
        (grads, weight_parts, node_features, x_mine, d_mine, gain_row, gain_mine, w_qkv),
        (
            shape((row_count, col_count), BF16),
            shape((3, share, col_count), F32),
        ),
        scratch=(
            pltpu.VMEM((width, 3 * col_count), BF16),
            pltpu.VMEM((head_count, row_count, col_count), BF16),
            pltpu.VMEM((others, row_count, col_count), BF16),
            pltpu.VMEM((block_count, 8, BLOCK), F32),
            pltpu.VMEM((others, block_count, 8, BLOCK), F32),
            pltpu.VMEM((seq_count - 1, 3, share, col_count), BF16),
            dma((others, chunks)),
            dma((others, chunks)),
            dma((others,)),
            dma((others,)),
            dma((seq_count - 1,)),
            dma((seq_count - 1,)),
        ),
        collective_id=0,
        has_side_effects=True,
    )
    return (layer_output, grad_input, grad_weights)


def solution(mesh):
    in_specs = (P("seq", None), P(), P(None, None, "head"), P("seq", None), P(), P("seq"))
    out_specs = (P("seq", "head"), P("seq", "head"), P(None, "seq", "head"))
    return jax.shard_map(shards, mesh=mesh, in_specs=in_specs, out_specs=out_specs, check_vma=False)
```
